32 devices in a mesh: ctx: 8 (over z, x), tp: 4 (over y, core).
Axes of the slice: x: 2, y: 2, z: 4, core: 2. Of those that a mesh axis runs over, the one named last changes fastest.
Arguments:
- tokens: bfloat16 [2048, 2048], P(('ctx', 'tp')), may hold values from -6 to 6
- w_query_key: bfloat16 [2, 2048, 2048], P(None, None, 'tp'), may hold values from -0.125 to 0.125
- w_value: bfloat16 [2048, 4096], P(None, 'tp'), may hold values from -0.125 to 0.125
- w_gate_out: bfloat16 [2048, 4096], P(None, 'tp'), may hold values from -0.125 to 0.125
- conv_query_key: float32 [2, 4, 2048], P(None, None, 'tp'), may hold values from -3 to 3
- conv_value: float32 [4, 4096], P(None, 'tp'), may hold values from -3 to 3
- log_decay: float32 [32, 2048], P('tp', 'ctx'), as said below
- beta: float32 [32, 2048], P('tp', 'ctx'), as said below
- seg_start: int32 [2048], P('ctx'), may hold values from 0 to 2047, as said below
- norm_gain: float32 [128], replicated, may hold values from 0.1 to 1.9
- w_output: bfloat16 [4096, 2048], P('tp'), may hold values from -0.09375 to 0.09375
Outputs:
- mixed: bfloat16 [2048, 2048], P(('ctx', 'tp'))
The draws below stay inside these ranges and needn't reach their ends.
Inputs may be any that keep to these rules, and one draw needn't show every extreme that they name: seg_start never falls along the tokens, seg_start[t] <= t, and seg_start[t] == t exactly at the first token of each rollout; two to five rollouts, the last token opening one of its own. log_decay <= 0. 0 < beta < 1.
All inputs are finite; a program needn't handle non-finite values.
Results may differ from the reference program's by a relative error of at most 0.014.
Values may be sent and summed in bfloat16 or wider, within the bound.
A program may use at most 64 MiB of HBM per device.

```python
import math
import jax
import jax.numpy as jnp
from jax import lax

D = 2048
HK = 16
DK = 128
VALUE_HEADS = 32
DV = 128
CONV = 4
STRETCH = 64
PACKED_TOKENS = 2048


def draw_log_decay(key, part):
    tier_key, variety_key, factor_key, locator_key, spike_run_key = jax.random.split(key, 5)
    slow_lo = math.log(0.1 / PACKED_TOKENS)
    slow_hi = math.log(1.0 / PACKED_TOKENS)
    slow = jnp.exp(jax.random.uniform(tier_key, (VALUE_HEADS, 1), jnp.float32, slow_lo, slow_hi))
    fast = jnp.exp(jax.random.uniform(variety_key, (VALUE_HEADS, 1), jnp.float32, math.log(1.0 / 50.0), math.log(1.0 / 20.0)))
    pick = jax.random.randint(jax.random.fold_in(variety_key, 7), (VALUE_HEADS, 1), 0, 2)
    tier_value = jnp.where(pick == 1, fast, slow)
    multiplier = jax.random.uniform(factor_key, (VALUE_HEADS, PACKED_TOKENS), jnp.float32, 0.5, 1.5)
    places = jax.random.randint(locator_key, (4,), 0, PACKED_TOKENS)
    matched_flag = jnp.any(jnp.arange(PACKED_TOKENS)[None, :] == places[:, None], axis=0)
    spike_run = jax.random.uniform(spike_run_key, (VALUE_HEADS, PACKED_TOKENS), jnp.float32, math.log(0.5), math.log(0.8))
    return (-tier_value * multiplier + jnp.where(matched_flag[None, :], spike_run, 0.0)).astype(jnp.float32)


def draw_beta(key, part):
    tier_key, factor_key = jax.random.split(key)
    tier_value = jnp.exp(jax.random.uniform(tier_key, (VALUE_HEADS, 1), jnp.float32, math.log(0.002), math.log(0.5)))
    multiplier = jax.random.uniform(factor_key, (VALUE_HEADS, PACKED_TOKENS), jnp.float32, 0.5, 1.5)
    return (tier_value * multiplier).astype(jnp.float32)


def draw_seg_start(key, part):
    random_cuts = jax.random.randint(key, (3,), 1, PACKED_TOKENS - 1)
    cuts = jnp.concatenate([random_cuts, jnp.full((1,), PACKED_TOKENS - 1, jnp.int32)]).astype(jnp.int32)
    position = jnp.arange(PACKED_TOKENS, dtype=jnp.int32)
    candidate = jnp.where(cuts[:, None] <= position[None, :], cuts[:, None], 0)
    return jnp.max(candidate, axis=0).astype(jnp.int32)


def block_levels(stream_key, dims, cuts, low, largest):
    loudness = 1.0
    for dim, parts in cuts:
        heights = jax.random.uniform(jax.random.fold_in(jax.random.fold_in(stream_key, 6), dim), (parts,), jnp.float32, low / len(cuts), largest / len(cuts))
        loudness = loudness * jnp.repeat(jnp.exp(heights), dims[dim] // parts).reshape((-1,) + (1,) * (len(dims) - 1 - dim))
    return loudness


def gaussian(rng, extent, deviation, limit, cuts=(), kind=jnp.bfloat16):
    loudness = block_levels(rng, extent, cuts, -0.22, 0.18) if cuts else 1.0
    values = jax.random.normal(rng, extent, jnp.float32) * deviation * loudness
    return jnp.minimum(jnp.maximum(values, -limit), limit).astype(kind)


def setup_inputs(seed: int = 0) -> dict:
    keys = jax.random.split(jax.random.key(seed), 12)
    return {
        "tokens": gaussian(keys[0], (PACKED_TOKENS, D), 1.0, 6.0, ((0, 32),)),
        "w_query_key": gaussian(keys[1], (2, D, HK * DK), D ** -0.5, 0.125, ((2, 4),)),
        "w_value": gaussian(keys[2], (D, VALUE_HEADS * DV), D ** -0.5, 0.125, ((1, 4),)),
        "w_gate_out": gaussian(keys[3], (D, VALUE_HEADS * DV), D ** -0.5, 0.125, ((1, 4),)),
        "conv_query_key": gaussian(keys[4], (2, CONV, HK * DK), 0.5, 3.0, ((2, 4),), jnp.float32),
        "conv_value": gaussian(keys[5], (CONV, VALUE_HEADS * DV), 0.5, 3.0, ((1, 4),), jnp.float32),
        "log_decay": draw_log_decay(jax.random.fold_in(keys[11], 71), 0),
        "beta": draw_beta(jax.random.fold_in(keys[11], 71), 0),
        "seg_start": draw_seg_start(jax.random.fold_in(keys[11], 71), 0),
        "norm_gain": jnp.clip(1.0 + 0.18 * jax.random.normal(keys[9], (DV,), jnp.float32), 0.1, 1.9),
        "w_output": gaussian(keys[10], (VALUE_HEADS * DV, D), (VALUE_HEADS * DV) ** -0.5, 0.09375, ((0, 4),)),
    }


highest = lax.Precision.HIGHEST

def stretch_parts(query, key, value, logd, betas, segs, first):
    size = segs.shape[0]
    gam = jnp.cumsum(logd, axis=-1)
    rows = jnp.arange(size)[:, None]
    cols = jnp.arange(size)[None, :]
    same = segs[:, None] == segs[None, :]
    within = jnp.logical_and(rows >= cols, same)
    strict = jnp.logical_and(rows > cols, same)
    gap = gam[:, :, None] - gam[:, None, :]
    decay = jnp.where(within, jnp.exp(jnp.where(within, gap, 0.0)), 0.0)
    lead = jnp.exp(gam) * (segs < first).astype(jnp.float32)
    keys_dot = jnp.einsum('hid,hjd->hij', key, key, precision=highest)
    lower_mat = jnp.eye(size, dtype=jnp.float32) + betas[:, :, None] * keys_dot * jnp.where(strict, decay, 0.0)
    w_one = lax.linalg.triangular_solve(lower_mat, betas[:, :, None] * value, left_side=True, lower=True, unit_diagonal=True)
    w_two = lax.linalg.triangular_solve(lower_mat, (betas * lead)[:, :, None] * key, left_side=True, lower=True, unit_diagonal=True)
    pmat = jnp.einsum('hid,hjd->hij', query, key, precision=highest) * decay
    local_out = jnp.einsum('hij,hjv->hiv', pmat, w_one, precision=highest)
    edge = lead[:, :, None] * query - jnp.einsum('hij,hjd->hid', pmat, w_two, precision=highest)
    tail = decay[:, -1, :]
    eye_key = jnp.eye(key.shape[-1], dtype=jnp.float32)
    mmat = lead[:, -1][:, None, None] * eye_key - jnp.einsum('hj,hjd,hje->hde', tail, w_two, key, precision=highest)
    bmat = jnp.einsum('hj,hjv,hjk->hvk', tail, w_one, key, precision=highest)
    return (local_out, edge, mmat, bmat)

def short_conv(pre, tail, weight, seg, position):
    extended = jnp.concatenate([tail, pre], axis=0).astype(jnp.float32)
    count = pre.shape[0]
    total = jnp.zeros((count, pre.shape[1]), jnp.float32)
    for j in range(CONV):
        reach = position - (CONV - 1) + j
        valid = (reach >= seg).astype(jnp.float32)[:, None]
        total = total + extended[j:j + count] * weight[j][None, :] * valid
    return jax.nn.silu(total)

def unit_norm(vecs):
    return vecs * lax.rsqrt(lax.optimization_barrier(jnp.sum(vecs * vecs, axis=-1, keepdims=True)) + 1e-06)

def reference(tokens, w_query_key, w_value, w_gate_out, conv_query_key, conv_value, log_decay, beta, seg_start, norm_gain, w_output):
    pre = jnp.concatenate([jnp.dot(tokens.astype(jnp.float32), w_query_key[0].astype(jnp.float32), preferred_element_type=jnp.float32), jnp.dot(tokens.astype(jnp.float32), w_query_key[1].astype(jnp.float32), preferred_element_type=jnp.float32), jnp.dot(tokens.astype(jnp.float32), w_value.astype(jnp.float32), preferred_element_type=jnp.float32)], axis=1).astype(jnp.bfloat16)
    gate_lin = jnp.dot(tokens.astype(jnp.float32), w_gate_out.astype(jnp.float32), preferred_element_type=jnp.float32)
    taps = jnp.concatenate([conv_query_key[0], conv_query_key[1], conv_value], axis=1)
    position = jnp.arange(PACKED_TOKENS, dtype=jnp.int32)
    empty_tail = jnp.zeros((CONV - 1, pre.shape[1]), jnp.bfloat16)
    act = short_conv(pre, empty_tail, taps, seg_start, position)
    width_qk = HK * DK
    query = unit_norm(act[:, :width_qk].reshape(PACKED_TOKENS, HK, DK)) * DK ** (-0.5)
    key = unit_norm(act[:, width_qk:2 * width_qk].reshape(PACKED_TOKENS, HK, DK))
    value = act[:, 2 * width_qk:].reshape(PACKED_TOKENS, VALUE_HEADS, DV)
    repeat = VALUE_HEADS // HK
    query = jnp.repeat(query, repeat, axis=1)
    key = jnp.repeat(key, repeat, axis=1)
    blocks = PACKED_TOKENS // STRETCH

    def arrange(field, depth):
        return field.reshape(blocks, STRETCH, VALUE_HEADS, depth).transpose(0, 2, 1, 3)
    logd = log_decay.reshape(VALUE_HEADS, blocks, STRETCH).transpose(1, 0, 2)
    betas = beta.reshape(VALUE_HEADS, blocks, STRETCH).transpose(1, 0, 2)
    segs = seg_start.reshape(blocks, STRETCH)
    firsts = (jnp.arange(blocks) * STRETCH).astype(jnp.int32)

    def advance(state, pieces):
        q_blk, k_blk, v_blk, l_blk, b_blk, s_blk, f_blk = pieces
        local_out, edge, mmat, bmat = stretch_parts(q_blk, k_blk, v_blk, l_blk, b_blk, s_blk, f_blk)
        result = local_out + jnp.einsum('hik,hvk->hiv', edge, state, precision=highest)
        state = jnp.einsum('hvk,hkl->hvl', state, mmat, precision=highest) + bmat
        return (state, result)
    start_state = jnp.zeros((VALUE_HEADS, DV, DK), jnp.float32)
    _, results = lax.scan(advance, start_state, (arrange(query, DK), arrange(key, DK), arrange(value, DV), logd, betas, segs, firsts))
    recur_out = results.transpose(0, 2, 1, 3).reshape(PACKED_TOKENS, VALUE_HEADS, DV)
    scale = lax.rsqrt(lax.optimization_barrier(jnp.mean(recur_out * recur_out, axis=-1, keepdims=True)) + 1e-06)
    normed = recur_out * scale * norm_gain * jax.nn.silu(gate_lin.reshape(PACKED_TOKENS, VALUE_HEADS, DV))
    normed = normed.reshape(PACKED_TOKENS, VALUE_HEADS * DV).astype(jnp.bfloat16)
    return jnp.dot(normed.astype(jnp.float32), w_output.astype(jnp.float32), preferred_element_type=jnp.float32).astype(jnp.bfloat16)
```

```python
import functools

import jax
import jax.numpy as jnp
from jax import lax
from jax.experimental import pallas as pl
from jax.experimental.pallas import tpu as pltpu
from jax.sharding import PartitionSpec as P

DK = 128
DV = 128
CONV = 4
TAIL = 16
HALF = 128

MESH = pl.DeviceIdType.MESH
F32 = jnp.float32
BF16 = jnp.bfloat16


def mm(a, b, dims=((1,), (0,))):
    return lax.dot_general(a, b, (dims, ((), ())), preferred_element_type=F32)


def halves(a):
    high = a.astype(BF16)
    return high, (a - high.astype(F32)).astype(BF16)


def mm3(a, b):
    a_high, a_low = halves(a)
    b_high, b_low = halves(b)
    return mm(a_high, b_high) + (mm(a_high, b_low) + mm(a_low, b_high))


def column(row):
    return jnp.broadcast_to(row, (8, row.shape[1])).T[:, :1]


def iota(shape, dim):
    return lax.broadcasted_iota(jnp.int32, shape, dim)


def silu(x):
    return x / (1.0 + jnp.exp(-x))


def level_of(size):
    diff = jnp.bitwise_xor(iota((size, size), 0), iota((size, size), 1))
    level = jnp.zeros((size, size), jnp.int32)
    for bit in range(size.bit_length() - 1):
        level = level + (diff >= (1 << bit)).astype(jnp.int32)
    return level


def unit_lower_inverse(lower, level, eye):
    size = lower.shape[0]
    inverse = eye - jnp.where(level == 1, lower, 0.0)
    for step in range(2, size.bit_length()):
        joint = jnp.where(level == step, lower, 0.0)
        inverse = inverse - mm3(mm3(inverse, joint), inverse)
    return inverse


def recurrence(
    devices,
    repeat,
    pre_ref,
    gate_ref,
    taps_ref,
    logd_ref,
    beta_ref,
    seg_ref,
    gain_ref,
    out_ref,
    ext,
    tail,
    level_ref,
    gam_ref,
    local_out,
    edge,
    mmat,
    bmat,
    outgoing,
    incoming,
    tail_sems,
    send_sems,
    recv_sems,
):
    me = lax.axis_index("ctx")
    not_first = me > 0
    not_last = me < devices - 1
    barrier = pltpu.get_barrier_semaphore()

    @pl.when(not_first)
    def _():
        pl.semaphore_signal(barrier, inc=1, device_id={"ctx": me - 1}, device_id_type=MESH)

    @pl.when(not_last)
    def _():
        pl.semaphore_signal(barrier, inc=1, device_id={"ctx": me + 1}, device_id_type=MESH)

    pl.semaphore_wait(barrier, not_first.astype(jnp.int32) + not_last.astype(jnp.int32))

    count, width = pre_ref.shape
    heads_v = logd_ref.shape[0]
    heads_k = heads_v // repeat
    width_qk = heads_k * DK
    tail_copy = pltpu.make_async_remote_copy(
        src_ref=pre_ref.at[pl.ds(count - TAIL, TAIL)],
        dst_ref=tail,
        send_sem=tail_sems.at[0],
        recv_sem=tail_sems.at[1],
        device_id={"ctx": me + 1},
        device_id_type=MESH,
    )

    @pl.when(not_last)
    def _():
        tail_copy.start()

    level_ref[...] = level_of(HALF)
    upper = (iota((count, count), 0) <= iota((count, count), 1)).astype(F32)
    gam_ref[...] = lax.dot_general(
        logd_ref[...], upper, (((1,), (0,)), ((), ())), precision=lax.Precision.HIGHEST,
        preferred_element_type=F32,
    )
    ext[TAIL:, :] = pre_ref[...].astype(F32)

    @pl.when(jnp.logical_not(not_first))
    def _():
        ext[:TAIL, :] = jnp.zeros((TAIL, width), F32)

    @pl.when(not_first)
    def _():
        tail_copy.wait_recv()
        ext[:TAIL, :] = tail[...].astype(F32)

    offset = me * count
    seg_row = seg_ref[...].astype(F32)
    seg_col = column(seg_row)
    position = (offset + iota((count, 1), 0)).astype(F32)
    since = position - seg_col
    valids = [(since >= float(CONV - 1 - j)).astype(F32) for j in range(CONV)]
    enters = (seg_col < offset.astype(F32)).astype(F32)
    same_last = seg_col == jnp.max(seg_row, axis=1, keepdims=True)

    def conv(at):
        lanes = pl.ds(pl.multiple_of(at, 128), 128)
        total = None
        for j in range(CONV):
            term = ext[TAIL - (CONV - 1) + j : TAIL - (CONV - 1) + j + count, lanes] * (
                taps_ref[j : j + 1, lanes] * valids[j]
            )
            total = term if total is None else total + term
        return silu(total)

    def unit(x):
        return x * lax.rsqrt(jnp.sum(x * x, axis=-1, keepdims=True) + 1e-06)

    def per_key_head(kh, carry):
        query = unit(conv(kh * DK)) * DK ** (-0.5)
        key = unit(conv(width_qk + kh * DK))
        key_b = key.astype(BF16)
        keys_dot = mm(key_b, key_b, ((1,), (1,)))
        query_dot = mm(query.astype(BF16), key_b, ((1,), (1,)))
        rows, cols = iota((count, count), 0), iota((count, count), 1)
        same = seg_col == seg_row
        within = jnp.logical_and(rows >= cols, same)
        strict = jnp.logical_and(rows > cols, same)
        eye = (iota((HALF, HALF), 0) == iota((HALF, HALF), 1)).astype(F32)
        eye_s = eye
        level = level_ref[...]
        for sub in range(repeat):
            h = kh * repeat + sub
            value = conv(2 * width_qk + h * DV)
            gam_row = gam_ref[pl.ds(h, 1), :]
            gam_col = column(gam_row)
            beta_col = column(beta_ref[pl.ds(h, 1), :])
            decay = jnp.where(within, jnp.exp(jnp.where(within, gam_col - gam_row, 0.0)), 0.0)
            lead = jnp.exp(gam_col) * enters
            lower = jnp.where(strict, beta_col * keys_dot * decay, 0.0)
            rhs = jnp.concatenate([beta_col * value, (beta_col * lead) * key], axis=1)
            solved = []
            for b in range(count // HALF):
                r = slice(b * HALF, (b + 1) * HALF)
                inverse = unit_lower_inverse(lower[r, r], level, eye)
                part = rhs[r]
                if solved:
                    before = solved[0] if b == 1 else jnp.concatenate(solved, axis=0)
                    part = part - mm3(lower[r, : b * HALF], before)
                solved.append(mm3(inverse, part))
            w_both = jnp.concatenate(solved, axis=0)
            w_both_b = w_both.astype(BF16)
            mixed = mm((query_dot * decay).astype(BF16), w_both_b)
            lanes = pl.ds(pl.multiple_of(h * DV, 128), DV)
            local_out[:, lanes] = mixed[:, :DV]
            edge[:, lanes] = (lead * query - mixed[:, DV:]).astype(BF16)
            gam_last = gam_row[:, count - 1 :]
            last = jnp.where(same_last, jnp.exp(jnp.where(same_last, gam_last - gam_col, 0.0)), 0.0)
            maps = mm((w_both * last).astype(BF16), key_b, ((0,), (0,)))
            bmat[h] = maps[:DV]
            mmat[h] = lead[count - 1 :, :] * eye_s - maps[DV:]
        return carry

    lax.fori_loop(0, heads_k, per_key_head, 0)

    def chain(h, carry):
        copy = pltpu.make_async_remote_copy(
            src_ref=outgoing.at[h],
            dst_ref=incoming.at[h],
            send_sem=send_sems.at[h],
            recv_sem=recv_sems.at[h],
            device_id={"ctx": me + 1},
            device_id_type=MESH,
        )

        @pl.when(not_first)
        def _():
            copy.wait_recv()

        @pl.when(jnp.logical_not(not_first))
        def _():
            incoming[h] = jnp.zeros((DV, DK), BF16)

        state = incoming[h]

        @pl.when(not_last)
        def _():
            map_high, map_low = halves(mmat[h])
            outgoing[h] = (mm(state, map_high) + mm(state, map_low) + bmat[h]).astype(BF16)
            copy.start()

        lanes = pl.ds(pl.multiple_of(h * DV, 128), DV)
        recur = local_out[:, lanes] + mm(edge[:, lanes], state, ((1,), (1,)))
        scale = lax.rsqrt(jnp.mean(recur * recur, axis=-1, keepdims=True) + 1e-06)
        out_ref[:, lanes] = (recur * scale * gain_ref[...] * silu(gate_ref[:, lanes])).astype(BF16)
        return carry

    lax.fori_loop(0, heads_v, chain, 0)

    @pl.when(not_last)
    def _():
        tail_copy.wait_send()

        def drain(h, carry):
            pltpu.make_async_remote_copy(
                src_ref=outgoing.at[h],
                dst_ref=incoming.at[h],
                send_sem=send_sems.at[h],
                recv_sem=recv_sems.at[h],
                device_id={"ctx": me + 1},
                device_id_type=MESH,
            ).wait_send()
            return carry

        lax.fori_loop(0, heads_v, drain, 0)


def local(
    devices,
    tokens,
    w_query_key,
    w_value,
    w_gate_out,
    conv_query_key,
    conv_value,
    log_decay,
    beta,
    seg_start,
    norm_gain,
    w_output,
):
    width_qk = w_query_key.shape[2]
    width_v = w_value.shape[1]
    heads_k = width_qk // DK
    heads_v = width_v // DV
    count = seg_start.shape[0]
    width = 2 * width_qk + width_v
    piece = lax.all_gather(tokens, "tp", axis=0, tiled=True)
    pre = jnp.concatenate(
        [
            jnp.dot(piece, w_query_key[0], preferred_element_type=F32).astype(BF16),
            jnp.dot(piece, w_query_key[1], preferred_element_type=F32).astype(BF16),
            jnp.dot(piece, w_value, preferred_element_type=F32).astype(BF16),
        ],
        axis=1,
    )
    gate_lin = jnp.dot(piece, w_gate_out, preferred_element_type=F32)
    taps = jnp.concatenate([conv_query_key[0], conv_query_key[1], conv_value], axis=1)
    vmem = pl.BlockSpec(memory_space=pltpu.VMEM)
    normed = pl.pallas_call(
        functools.partial(recurrence, devices, heads_v // heads_k),
        out_shape=jax.ShapeDtypeStruct((count, width_v), BF16),
        in_specs=[vmem] * 7,
        out_specs=vmem,
        scratch_shapes=[
            pltpu.VMEM((TAIL + count, width), F32),
            pltpu.VMEM((TAIL, width), BF16),
            pltpu.VMEM((HALF, HALF), jnp.int32),
            pltpu.VMEM((heads_v, count), F32),
            pltpu.VMEM((count, width_v), F32),
            pltpu.VMEM((count, width_v), BF16),
            pltpu.VMEM((heads_v, DK, DK), F32),
            pltpu.VMEM((heads_v, DV, DK), F32),
            pltpu.VMEM((heads_v, DV, DK), BF16),
            pltpu.VMEM((heads_v, DV, DK), BF16),
            pltpu.SemaphoreType.DMA((2,)),
            pltpu.SemaphoreType.DMA((heads_v,)),
            pltpu.SemaphoreType.DMA((heads_v,)),
        ],
        compiler_params=pltpu.CompilerParams(
            collective_id=0, has_side_effects=True, vmem_limit_bytes=48 << 20
        ),
    )(pre, gate_lin, taps, log_decay, beta, seg_start.reshape(1, count), norm_gain.reshape(1, DV))
    return lax.psum_scatter(
        jnp.dot(normed, w_output, preferred_element_type=F32).astype(BF16),
        "tp",
        scatter_dimension=0,
        tiled=True,
    )


def solution(mesh):
    return jax.shard_map(
        functools.partial(local, mesh.shape["ctx"]),
        mesh=mesh,
        in_specs=(
            P(("ctx", "tp"), None),
            P(None, None, "tp"),
            P(None, "tp"),
            P(None, "tp"),
            P(None, None, "tp"),
            P(None, "tp"),
            P("tp", "ctx"),
            P("tp", "ctx"),
            P("ctx"),
            P(),
            P("tp", None),
        ),
        out_specs=P(("ctx", "tp"), None),
        check_vma=False,
    )
```

```python
import functools

import jax
import jax.numpy as jnp
from jax import lax
from jax.experimental import pallas as pl
from jax.experimental.pallas import tpu as pltpu
from jax.sharding import PartitionSpec as P

DK = 128
DV = 128
CONV = 4
TAIL = 16
HALF = 128
TILE = 256
OUT_TILE = 512

MESH = pl.DeviceIdType.MESH
F32 = jnp.float32
BF16 = jnp.bfloat16


def mm(a, b, dims=((1,), (0,))):
    return lax.dot_general(a, b, (dims, ((), ())), preferred_element_type=F32)


def halves(a):
    high = a.astype(BF16)
    return high, (a - high.astype(F32)).astype(BF16)


def mm3(a, b):
    a_high, a_low = halves(a)
    b_high, b_low = halves(b)
    return mm(a_high, b_high) + (mm(a_high, b_low) + mm(a_low, b_high))


def column(row):
    return jnp.broadcast_to(row, (8, row.shape[1])).T[:, :1]


def iota(shape, dim):
    return lax.broadcasted_iota(jnp.int32, shape, dim)


def silu(x):
    return x / (1.0 + jnp.exp(-x))


def level_of(size):
    diff = jnp.bitwise_xor(iota((size, size), 0), iota((size, size), 1))
    level = jnp.zeros((size, size), jnp.int32)
    for bit in range(size.bit_length() - 1):
        level = level + (diff >= (1 << bit)).astype(jnp.int32)
    return level


def unit_lower_inverse(lower, level, eye):
    size = lower.shape[0]
    inverse = eye - jnp.where(level == 1, lower, 0.0)
    for step in range(2, size.bit_length()):
        joint = jnp.where(level == step, lower, 0.0)
        inverse = inverse - mm3(mm3(inverse, joint), inverse)
    return inverse


def layer(
    devices,
    peers,
    repeat,
    tokens_ref,
    taps_ref,
    logd_ref,
    beta_ref,
    seg_ref,
    gain_ref,
    w_query_key_hbm,
    w_value_hbm,
    w_gate_hbm,
    w_output_hbm,
    out_ref,
    w_query_key,
    w_value,
    w_gate,
    w_output,
    gathered,
    tail_out,
    gate_ref,
    normed,
    ext,
    tail,
    level_ref,
    gam_ref,
    local_out,
    edge,
    mmat,
    bmat,
    outgoing,
    incoming,
    core_out,
    core_in,
    chip_out,
    chip_in,
    total,
    weight_sems,
    tail_sems,
    send_sems,
    recv_sems,
    gather_send,
    gather_recv,
    pass_send,
    pass_recv,
    core_send,
    core_recv,
    chip_send,
    chip_recv,
):
    me = lax.axis_index("ctx")
    slot = lax.axis_index("tp")
    core, chip, chips = slot % 2, slot // 2, peers // 2
    partner = chip * 2 + 1 - core
    not_first = me > 0
    not_last = me < devices - 1
    rows, depth = tokens_ref.shape
    count = rows * peers
    heads_v = logd_ref.shape[0]
    heads_k = heads_v // repeat
    width_qk = heads_k * DK
    width_v = heads_v * DV
    width = 2 * width_qk + width_v

    loads = [
        pltpu.make_async_copy(src, dst, weight_sems.at[n])
        for n, (src, dst) in enumerate(
            [
                (w_query_key_hbm, w_query_key),
                (w_value_hbm, w_value),
                (w_gate_hbm, w_gate),
                (w_output_hbm, w_output),
            ]
        )
    ]
    for load in loads:
        load.start()

    def chip_at(d):
        return lax.rem(chip + d, chips)

    def on_chip(d):
        return {"tp": chip_at(d) * 2 + core}

    barrier = pltpu.get_barrier_semaphore()

    @pl.when(not_first)
    def _():
        pl.semaphore_signal(barrier, inc=1, device_id={"ctx": me - 1}, device_id_type=MESH)

    @pl.when(not_last)
    def _():
        pl.semaphore_signal(barrier, inc=1, device_id={"ctx": me + 1}, device_id_type=MESH)

    pl.semaphore_signal(barrier, inc=1, device_id={"tp": partner}, device_id_type=MESH)
    for d in range(1, chips):
        pl.semaphore_signal(barrier, inc=1, device_id=on_chip(d), device_id_type=MESH)
    pl.semaphore_wait(barrier, not_first.astype(jnp.int32) + not_last.astype(jnp.int32) + chips)

    def remote(src, dst, send, recv, device):
        return pltpu.make_async_remote_copy(
            src_ref=src, dst_ref=dst, send_sem=send, recv_sem=recv, device_id=device, device_id_type=MESH
        )

    def block(index):
        return gathered.at[pl.ds(pl.multiple_of(index * rows, 16), rows)]

    across = [
        remote(tokens_ref, block(slot), gather_send.at[d], gather_recv.at[d], on_chip(d))
        for d in range(1, chips)
    ]
    for copy in across:
        copy.start()
    passes = [remote(tokens_ref, block(slot), pass_send.at[0], pass_recv.at[0], {"tp": partner})]
    passes[0].start()
    gathered[pl.ds(pl.multiple_of(slot * rows, 16), rows), :] = tokens_ref[...]

    level_ref[...] = level_of(HALF)
    upper = (iota((count, count), 0) <= iota((count, count), 1)).astype(F32)
    gam_ref[...] = lax.dot_general(
        logd_ref[...], upper, (((1,), (0,)), ((), ())), precision=lax.Precision.HIGHEST,
        preferred_element_type=F32,
    )

    for d in range(1, chips):
        across[d - 1].wait_recv()
        came = chip_at(chips - d) * 2 + core
        passes.append(remote(block(came), block(came), pass_send.at[d], pass_recv.at[d], {"tp": partner}))
        passes[d].start()
    for copy in passes:
        copy.wait_recv()

    def project_pre(weight, first, columns):
        def tile(t, carry):
            lanes = pl.ds(pl.multiple_of(t * TILE, TILE), TILE)
            to = pl.ds(pl.multiple_of(first + t * TILE, TILE), TILE)
            part = mm(gathered[...], weight[:, lanes]).astype(BF16)
            ext[TAIL:, to] = part.astype(F32)
            tail_out[:, to] = part[count - TAIL :]
            return carry

        lax.fori_loop(0, columns // TILE, tile, 0)

    loads[0].wait()
    project_pre(w_query_key.at[0], 0, width_qk)
    project_pre(w_query_key.at[1], width_qk, width_qk)
    loads[1].wait()
    project_pre(w_value, 2 * width_qk, width_v)

    tail_copy = remote(tail_out, tail, tail_sems.at[0], tail_sems.at[1], {"ctx": me + 1})

    @pl.when(not_last)
    def _():
        tail_copy.start()

    loads[2].wait()

    def project_gate(t, carry):
        lanes = pl.ds(pl.multiple_of(t * TILE, TILE), TILE)
        gate_ref[:, lanes] = mm(gathered[...], w_gate[:, lanes])
        return carry

    lax.fori_loop(0, width_v // TILE, project_gate, 0)

    @pl.when(jnp.logical_not(not_first))
    def _():
        ext[:TAIL, :] = jnp.zeros((TAIL, width), F32)

    @pl.when(not_first)
    def _():
        tail_copy.wait_recv()
        ext[:TAIL, :] = tail[...].astype(F32)

    offset = me * count
    seg_row = seg_ref[...].astype(F32)
    seg_col = column(seg_row)
    position = (offset + iota((count, 1), 0)).astype(F32)
    since = position - seg_col
    valids = [(since >= float(CONV - 1 - j)).astype(F32) for j in range(CONV)]
    enters = (seg_col < offset.astype(F32)).astype(F32)
    same_last = seg_col == jnp.max(seg_row, axis=1, keepdims=True)

    def conv(at):
        lanes = pl.ds(pl.multiple_of(at, 128), 128)
        total = None
        for j in range(CONV):
            term = ext[TAIL - (CONV - 1) + j : TAIL - (CONV - 1) + j + count, lanes] * (
                taps_ref[j : j + 1, lanes] * valids[j]
            )
            total = term if total is None else total + term
        return silu(total)

    def unit(x):
        return x * lax.rsqrt(jnp.sum(x * x, axis=-1, keepdims=True) + 1e-06)

    def per_key_head(kh, carry):
        query = unit(conv(kh * DK)) * DK ** (-0.5)
        key = unit(conv(width_qk + kh * DK))
        key_b = key.astype(BF16)
        keys_dot = mm(key_b, key_b, ((1,), (1,)))
        query_dot = mm(query.astype(BF16), key_b, ((1,), (1,)))
        rows, cols = iota((count, count), 0), iota((count, count), 1)
        same = seg_col == seg_row
        within = jnp.logical_and(rows >= cols, same)
        strict = jnp.logical_and(rows > cols, same)
        eye = (iota((HALF, HALF), 0) == iota((HALF, HALF), 1)).astype(F32)
        eye_s = eye
        level = level_ref[...]
        for sub in range(repeat):
            h = kh * repeat + sub
            value = conv(2 * width_qk + h * DV)
            gam_row = gam_ref[pl.ds(h, 1), :]
            gam_col = column(gam_row)
            beta_col = column(beta_ref[pl.ds(h, 1), :])
            decay = jnp.where(within, jnp.exp(jnp.where(within, gam_col - gam_row, 0.0)), 0.0)
            lead = jnp.exp(gam_col) * enters
            lower = jnp.where(strict, beta_col * keys_dot * decay, 0.0)
            rhs = jnp.concatenate([beta_col * value, (beta_col * lead) * key], axis=1)
            solved = []
            for b in range(count // HALF):
                r = slice(b * HALF, (b + 1) * HALF)
                inverse = unit_lower_inverse(lower[r, r], level, eye)
                part = rhs[r]
                if solved:
                    before = solved[0] if b == 1 else jnp.concatenate(solved, axis=0)
                    part = part - mm3(lower[r, : b * HALF], before)
                solved.append(mm3(inverse, part))
            w_both = jnp.concatenate(solved, axis=0)
            w_both_b = w_both.astype(BF16)
            mixed = mm((query_dot * decay).astype(BF16), w_both_b)
            lanes = pl.ds(pl.multiple_of(h * DV, 128), DV)
            local_out[:, lanes] = mixed[:, :DV]
            edge[:, lanes] = (lead * query - mixed[:, DV:]).astype(BF16)
            gam_last = gam_row[:, count - 1 :]
            last = jnp.where(same_last, jnp.exp(jnp.where(same_last, gam_last - gam_col, 0.0)), 0.0)
            maps = mm((w_both * last).astype(BF16), key_b, ((0,), (0,)))
            bmat[h] = maps[:DV]
            mmat[h] = lead[count - 1 :, :] * eye_s - maps[DV:]
        return carry

    lax.fori_loop(0, heads_k, per_key_head, 0)

    def chain(h, carry):
        copy = pltpu.make_async_remote_copy(
            src_ref=outgoing.at[h],
            dst_ref=incoming.at[h],
            send_sem=send_sems.at[h],
            recv_sem=recv_sems.at[h],
            device_id={"ctx": me + 1},
            device_id_type=MESH,
        )

        @pl.when(not_first)
        def _():
            copy.wait_recv()

        @pl.when(jnp.logical_not(not_first))
        def _():
            incoming[h] = jnp.zeros((DV, DK), BF16)

        state = incoming[h]

        @pl.when(not_last)
        def _():
            map_high, map_low = halves(mmat[h])
            outgoing[h] = (mm(state, map_high) + mm(state, map_low) + bmat[h]).astype(BF16)
            copy.start()

        lanes = pl.ds(pl.multiple_of(h * DV, 128), DV)
        recur = local_out[:, lanes] + mm(edge[:, lanes], state, ((1,), (1,)))
        scale = lax.rsqrt(jnp.mean(recur * recur, axis=-1, keepdims=True) + 1e-06)
        normed[:, lanes] = (recur * scale * gain_ref[...] * silu(gate_ref[:, lanes])).astype(BF16)
        return carry

    lax.fori_loop(0, heads_v, chain, 0)

    loads[3].wait()
    tiles = depth // OUT_TILE

    def rows_for(which):
        return jnp.concatenate(
            [
                normed[pl.ds(pl.multiple_of((chip_at(d) * 2 + which) * rows, 16), rows), :]
                for d in range(chips)
            ],
            axis=0,
        )

    def core_copy(t):
        return remote(core_out.at[t], core_in.at[t], core_send.at[t], core_recv.at[t], {"tp": partner})

    def chip_copy(t, d):
        return remote(
            chip_out.at[t, d - 1], chip_in.at[t, d - 1], chip_send.at[t, d - 1], chip_recv.at[t, d - 1], on_chip(d)
        )

    def for_partner(t, carry):
        lanes = pl.ds(pl.multiple_of(t * OUT_TILE, OUT_TILE), OUT_TILE)
        core_out[t] = mm(rows_for(1 - core), w_output[:, lanes]).astype(BF16)
        core_copy(t).start()
        return carry

    lax.fori_loop(0, tiles, for_partner, 0)

    def for_core(t, carry):
        lanes = pl.ds(pl.multiple_of(t * OUT_TILE, OUT_TILE), OUT_TILE)
        part = mm(rows_for(core), w_output[:, lanes])
        core_copy(t).wait_recv()
        part = part + core_in[t].astype(F32)
        for d in range(1, chips):
            chip_out[t, d - 1] = part[d * rows : (d + 1) * rows].astype(BF16)
            chip_copy(t, d).start()
        total[:, lanes] = part[:rows]
        return carry

    lax.fori_loop(0, tiles, for_core, 0)

    def finish(t, carry):
        lanes = pl.ds(pl.multiple_of(t * OUT_TILE, OUT_TILE), OUT_TILE)
        part = total[:, lanes]
        for d in range(1, chips):
            chip_copy(t, d).wait_recv()
            part = part + chip_in[t, d - 1].astype(F32)
        out_ref[:, lanes] = part.astype(BF16)
        return carry

    lax.fori_loop(0, tiles, finish, 0)

    for copy in across + passes:
        copy.wait_send()

    def drain_sums(t, carry):
        core_copy(t).wait_send()
        for d in range(1, chips):
            chip_copy(t, d).wait_send()
        return carry

    lax.fori_loop(0, tiles, drain_sums, 0)

    @pl.when(not_last)
    def _():
        tail_copy.wait_send()

        def drain(h, carry):
            pltpu.make_async_remote_copy(
                src_ref=outgoing.at[h],
                dst_ref=incoming.at[h],
                send_sem=send_sems.at[h],
                recv_sem=recv_sems.at[h],
                device_id={"ctx": me + 1},
                device_id_type=MESH,
            ).wait_send()
            return carry

        lax.fori_loop(0, heads_v, drain, 0)


def local(
    devices,
    peers,
    tokens,
    w_query_key,
    w_value,
    w_gate_out,
    conv_query_key,
    conv_value,
    log_decay,
    beta,
    seg_start,
    norm_gain,
    w_output,
):
    width_qk = w_query_key.shape[2]
    width_v = w_value.shape[1]
    heads_k = width_qk // DK
    heads_v = width_v // DV
    count = seg_start.shape[0]
    rows, depth = tokens.shape
    width = 2 * width_qk + width_v
    chips = peers // 2
    others = max(chips - 1, 1)
    tiles = depth // OUT_TILE
    taps = jnp.concatenate([conv_query_key[0], conv_query_key[1], conv_value], axis=1)
    vmem = pl.BlockSpec(memory_space=pltpu.VMEM)
    anywhere = pl.BlockSpec(memory_space=pl.ANY)
    dma = pltpu.SemaphoreType.DMA
    return pl.pallas_call(
        functools.partial(layer, devices, peers, heads_v // heads_k),
        out_shape=jax.ShapeDtypeStruct((rows, depth), BF16),
        in_specs=[vmem] * 6 + [anywhere] * 4,
        out_specs=vmem,
        scratch_shapes=[
            pltpu.VMEM(w_query_key.shape, BF16),
            pltpu.VMEM(w_value.shape, BF16),
            pltpu.VMEM(w_gate_out.shape, BF16),
            pltpu.VMEM(w_output.shape, BF16),
            pltpu.VMEM((count, depth), BF16),
            pltpu.VMEM((TAIL, width), BF16),
            pltpu.VMEM((count, width_v), F32),
            pltpu.VMEM((count, width_v), BF16),
            pltpu.VMEM((TAIL + count, width), F32),
            pltpu.VMEM((TAIL, width), BF16),
            pltpu.VMEM((HALF, HALF), jnp.int32),
            pltpu.VMEM((heads_v, count), F32),
            pltpu.VMEM((count, width_v), F32),
            pltpu.VMEM((count, width_v), BF16),
            pltpu.VMEM((heads_v, DK, DK), F32),
            pltpu.VMEM((heads_v, DV, DK), F32),
            pltpu.VMEM((heads_v, DV, DK), BF16),
            pltpu.VMEM((heads_v, DV, DK), BF16),
            pltpu.VMEM((tiles, chips * rows, OUT_TILE), BF16),
            pltpu.VMEM((tiles, chips * rows, OUT_TILE), BF16),
            pltpu.VMEM((tiles, others, rows, OUT_TILE), BF16),
            pltpu.VMEM((tiles, others, rows, OUT_TILE), BF16),
            pltpu.VMEM((rows, depth), F32),
            dma((4,)),
            dma((2,)),
            dma((heads_v,)),
            dma((heads_v,)),
            dma((chips,)),
            dma((chips,)),
            dma((chips,)),
            dma((chips,)),
            dma((tiles,)),
            dma((tiles,)),
            dma((tiles, others)),
            dma((tiles, others)),
        ],
        compiler_params=pltpu.CompilerParams(
            collective_id=0, has_side_effects=True, vmem_limit_bytes=56 << 20
        ),
    )(
        tokens,
        taps,
        log_decay,
        beta,
        seg_start.reshape(1, count),
        norm_gain.reshape(1, DV),
        w_query_key,
        w_value,
        w_gate_out,
        w_output,
    )


def solution(mesh):
    return jax.shard_map(
        functools.partial(local, mesh.shape["ctx"], mesh.shape["tp"]),
        mesh=mesh,
        in_specs=(
            P(("ctx", "tp"), None),
            P(None, None, "tp"),
            P(None, "tp"),
            P(None, "tp"),
            P(None, None, "tp"),
            P(None, "tp"),
            P("tp", "ctx"),
            P("tp", "ctx"),
            P("ctx"),
            P(),
            P("tp", None),
        ),
        out_specs=P(("ctx", "tp"), None),
        check_vma=False,
    )
```

```python
import functools

import jax
import jax.numpy as jnp
from jax import lax
from jax.experimental import pallas as pl
from jax.experimental.pallas import tpu as pltpu
from jax.sharding import PartitionSpec as P

DK = 128
DV = 128
CONV = 4
TAIL = 16
HALF = 128
TILE = 256
OUT_TILE = 512

MESH = pl.DeviceIdType.MESH
F32 = jnp.float32
BF16 = jnp.bfloat16


def mm(a, b, dims=((1,), (0,))):
    return lax.dot_general(a, b, (dims, ((), ())), preferred_element_type=F32)


def halves(a):
    high = a.astype(BF16)
    return high, (a - high.astype(F32)).astype(BF16)


def mm3(a, b):
    a_high, a_low = halves(a)
    b_high, b_low = halves(b)
    return mm(a_high, b_high) + (mm(a_high, b_low) + mm(a_low, b_high))


def column(row):
    return jnp.broadcast_to(row, (8, row.shape[1])).T[:, :1]


def iota(shape, dim):
    return lax.broadcasted_iota(jnp.int32, shape, dim)


def silu(x):
    return x / (1.0 + jnp.exp(-x))


def level_of(size):
    diff = jnp.bitwise_xor(iota((size, size), 0), iota((size, size), 1))
    level = jnp.zeros((size, size), jnp.int32)
    for bit in range(size.bit_length() - 1):
        level = level + (diff >= (1 << bit)).astype(jnp.int32)
    return level


def unit_lower_inverses(lowers, level, eye):
    size = lowers[0].shape[0]
    inverses = [eye - jnp.where(level == 1, lower, 0.0) for lower in lowers]
    for step in range(2, size.bit_length()):
        joints = [jnp.where(level == step, lower, 0.0).astype(BF16) for lower in lowers]
        rounded = [inverse.astype(BF16) for inverse in inverses]
        firsts = [mm(x, joint).astype(BF16) for x, joint in zip(rounded, joints)]
        seconds = [mm(first, x) for first, x in zip(firsts, rounded)]
        inverses = [inverse - second for inverse, second in zip(inverses, seconds)]
    rests = [eye - inverse - mm3(lower, inverse) for lower, inverse in zip(lowers, inverses)]
    return [inverse + mm(inverse.astype(BF16), rest.astype(BF16)) for inverse, rest in zip(inverses, rests)]


def layer(
    devices,
    peers,
    repeat,
    tokens_ref,
    taps_query_key,
    taps_value,
    logd_ref,
    beta_ref,
    seg_ref,
    gain_ref,
    w_query_key_hbm,
    w_value_hbm,
    w_gate_hbm,
    w_output_hbm,
    out_ref,
    w_query_key,
    w_value,
    w_gate,
    w_output,
    gathered,
    tail_out,
    gate_ref,
    normed,
    ext,
    tail,
    level_ref,
    gam_ref,
    keys,
    decays,
    corrected,
    map_high,
    map_low,
    bmat,
    outgoing,
    incoming,
    core_out,
    core_in,
    chip_out,
    chip_in,
    total,
    weight_sems,
    tail_sems,
    send_sems,
    recv_sems,
    gather_send,
    gather_recv,
    pass_send,
    pass_recv,
    core_send,
    core_recv,
    chip_send,
    chip_recv,
):
    me = lax.axis_index("ctx")
    slot = lax.axis_index("tp")
    core, chip, chips = slot % 2, slot // 2, peers // 2
    partner = chip * 2 + 1 - core
    not_first = me > 0
    not_last = me < devices - 1
    rows, depth = tokens_ref.shape
    count = rows * peers
    heads_v = logd_ref.shape[0]
    heads_k = heads_v // repeat
    width_qk = heads_k * DK
    width_v = heads_v * DV
    width = 2 * width_qk + width_v

    loads = [
        pltpu.make_async_copy(src, dst, weight_sems.at[n])
        for n, (src, dst) in enumerate(
            [
                (w_query_key_hbm, w_query_key),
                (w_value_hbm, w_value),
                (w_gate_hbm, w_gate),
                (w_output_hbm, w_output),
            ]
        )
    ]
    for load in loads:
        load.start()

    def chip_at(d):
        return lax.rem(chip + d, chips)

    def on_chip(d):
        return {"tp": chip_at(d) * 2 + core}

    barrier = pltpu.get_barrier_semaphore()

    @pl.when(not_first)
    def _():
        pl.semaphore_signal(barrier, inc=1, device_id={"ctx": me - 1}, device_id_type=MESH)

    @pl.when(not_last)
    def _():
        pl.semaphore_signal(barrier, inc=1, device_id={"ctx": me + 1}, device_id_type=MESH)

    pl.semaphore_signal(barrier, inc=1, device_id={"tp": partner}, device_id_type=MESH)
    for d in range(1, chips):
        pl.semaphore_signal(barrier, inc=1, device_id=on_chip(d), device_id_type=MESH)
    pl.semaphore_wait(barrier, not_first.astype(jnp.int32) + not_last.astype(jnp.int32) + chips)

    def remote(src, dst, send, recv, device):
        return pltpu.make_async_remote_copy(
            src_ref=src, dst_ref=dst, send_sem=send, recv_sem=recv, device_id=device, device_id_type=MESH
        )

    def block(index):
        return gathered.at[pl.ds(pl.multiple_of(index * rows, 16), rows)]

    across = [
        remote(tokens_ref, block(slot), gather_send.at[d], gather_recv.at[d], on_chip(d))
        for d in range(1, chips)
    ]
    for copy in across:
        copy.start()
    passes = [remote(tokens_ref, block(slot), pass_send.at[0], pass_recv.at[0], {"tp": partner})]
    passes[0].start()
    gathered[pl.ds(pl.multiple_of(slot * rows, 16), rows), :] = tokens_ref[...]

    level_ref[...] = level_of(HALF)
    upper = (iota((count, count), 0) <= iota((count, count), 1)).astype(F32)
    gam_ref[...] = lax.dot_general(
        logd_ref[...], upper, (((1,), (0,)), ((), ())), precision=lax.Precision.HIGHEST,
        preferred_element_type=F32,
    )

    for d in range(1, chips):
        across[d - 1].wait_recv()
        came = chip_at(chips - d) * 2 + core
        passes.append(remote(block(came), block(came), pass_send.at[d], pass_recv.at[d], {"tp": partner}))
        passes[d].start()
    for copy in passes:
        copy.wait_recv()

    def project_pre(weight, first, columns):
        def tile(t, carry):
            lanes = pl.ds(pl.multiple_of(t * TILE, TILE), TILE)
            to = pl.ds(pl.multiple_of(first + t * TILE, TILE), TILE)
            part = mm(gathered[...], weight[:, lanes]).astype(BF16)
            ext[TAIL:, to] = part.astype(F32)
            tail_out[:, to] = part[count - TAIL :]
            return carry

        lax.fori_loop(0, columns // TILE, tile, 0)

    loads[0].wait()
    project_pre(w_query_key.at[0], 0, width_qk)
    project_pre(w_query_key.at[1], width_qk, width_qk)
    loads[1].wait()
    project_pre(w_value, 2 * width_qk, width_v)

    tail_copy = remote(tail_out, tail, tail_sems.at[0], tail_sems.at[1], {"ctx": me + 1})

    @pl.when(not_last)
    def _():
        tail_copy.start()

    loads[2].wait()

    def project_gate(t, carry):
        lanes = pl.ds(pl.multiple_of(t * TILE, TILE), TILE)
        gate_ref[:, lanes] = mm(gathered[...], w_gate[:, lanes])
        return carry

    lax.fori_loop(0, width_v // TILE, project_gate, 0)

    @pl.when(jnp.logical_not(not_first))
    def _():
        ext[:TAIL, :] = jnp.zeros((TAIL, width), F32)

    @pl.when(not_first)
    def _():
        tail_copy.wait_recv()
        ext[:TAIL, :] = tail[...].astype(F32)

    offset = me * count
    seg_row = seg_ref[...].astype(F32)
    seg_col = column(seg_row)
    position = (offset + iota((count, 1), 0)).astype(F32)
    since = position - seg_col
    valids = [(since >= float(CONV - 1 - j)).astype(F32) for j in range(CONV)]
    enters = (seg_col < offset.astype(F32)).astype(F32)
    same_last = seg_col == jnp.max(seg_row, axis=1, keepdims=True)

    def conv(at, taps_ref, tap_at):
        lanes = pl.ds(pl.multiple_of(at, 128), 128)
        tap_lanes = pl.ds(pl.multiple_of(tap_at, 128), 128)
        total = None
        for j in range(CONV):
            term = ext[TAIL - (CONV - 1) + j : TAIL - (CONV - 1) + j + count, lanes] * (
                taps_ref[j : j + 1, tap_lanes] * valids[j]
            )
            total = term if total is None else total + term
        return silu(total)

    def unit(x):
        return x * lax.rsqrt(jnp.sum(x * x, axis=-1, keepdims=True) + 1e-06)

    def state_copy(g):
        return remote(outgoing.at[g], incoming.at[g], send_sems.at[g], recv_sems.at[g], {"ctx": me + 1})

    def head_lanes(h):
        return pl.ds(pl.multiple_of(h * DV, 128), DV)

    def pass_state(g):
        @pl.when(not_first)
        def _():
            state_copy(g).wait_recv()

        @pl.when(jnp.logical_not(not_first))
        def _():
            incoming[g] = jnp.zeros((repeat * DV, DK), BF16)

        @pl.when(not_last)
        def _():
            for sub in range(repeat):
                h = g * repeat + sub
                part = slice(sub * DV, (sub + 1) * DV)
                state = incoming[g, part, :]
                outgoing[g, part, :] = (mm(state, map_high[h]) + mm(state, map_low[h]) + bmat[h]).astype(BF16)
            state_copy(g).start()

    ahead = jnp.minimum(me, heads_k)
    eye = (iota((HALF, HALF), 0) == iota((HALF, HALF), 1)).astype(F32)
    parts = [slice(b * HALF, (b + 1) * HALF) for b in range(count // HALF)]

    def key_side(g, carry):
        key = unit(conv(width_qk + g * DK, taps_query_key.at[1], g * DK))
        key_b = key.astype(BF16)
        keys[:, head_lanes(g)] = key_b
        keys_dot = mm(key_b, key_b, ((1,), (1,)))
        rows_i, cols_i = iota((count, count), 0), iota((count, count), 1)
        within = jnp.logical_and(rows_i >= cols_i, seg_col == seg_row)
        strict = jnp.logical_and(rows_i > cols_i, within)
        level = level_ref[...]
        lowers, sides, lasts, leads = [], [], [], []
        for sub in range(repeat):
            h = g * repeat + sub
            value = conv(2 * width_qk + h * DV, taps_value, h * DV)
            gam_row = gam_ref[pl.ds(h, 1), :]
            gam_col = column(gam_row)
            beta_col = column(beta_ref[pl.ds(h, 1), :])
            decay = jnp.where(within, jnp.exp(jnp.where(within, gam_col - gam_row, 0.0)), 0.0)
            decays[h] = decay
            lead = jnp.exp(gam_col) * enters
            lowers.append(jnp.where(strict, beta_col * keys_dot * decay, 0.0))
            sides.append(jnp.concatenate([beta_col * value, (beta_col * lead) * key], axis=1))
            gam_last = gam_row[:, count - 1 :]
            lasts.append(jnp.where(same_last, jnp.exp(jnp.where(same_last, gam_last - gam_col, 0.0)), 0.0))
            leads.append(lead[count - 1 :, :])
        inverses = unit_lower_inverses([lower[r, r] for lower in lowers for r in parts], level, eye)
        solved = [[] for _ in range(repeat)]
        for b, r in enumerate(parts):
            for sub in range(repeat):
                part = sides[sub][r]
                if b:
                    part = part - mm3(lowers[sub][r, : b * HALF], jnp.concatenate(solved[sub], axis=0))
                solved[sub].append(mm3(inverses[sub * len(parts) + b], part))
        for sub in range(repeat):
            h = g * repeat + sub
            w_both = jnp.concatenate(solved[sub], axis=0)
            corrected[h] = w_both.astype(BF16)
            maps = mm((w_both * lasts[sub]).astype(BF16), key_b, ((0,), (0,)))
            bmat[h] = maps[:DV]
            map_high[h], map_low[h] = halves(leads[sub] * eye - maps[DV:])

        @pl.when(g >= ahead)
        def _():
            pass_state(g - ahead)

        return carry

    lax.fori_loop(0, heads_k, key_side, 0)

    def query_side(g, carry):
        query = unit(conv(g * DK, taps_query_key.at[0], g * DK)) * DK ** (-0.5)
        query_dot = mm(query.astype(BF16), keys[:, head_lanes(g)], ((1,), (1,)))
        firsts, edges = [], []
        for sub in range(repeat):
            h = g * repeat + sub
            lead = jnp.exp(column(gam_ref[pl.ds(h, 1), :])) * enters
            both = mm((query_dot * decays[h]).astype(BF16), corrected[h])
            firsts.append(both[:, :DV])
            edges.append((lead * query - both[:, DV:]).astype(BF16))

        @pl.when(g >= heads_k - ahead)
        def _():
            pass_state(g)

        for sub in range(repeat):
            lanes = head_lanes(g * repeat + sub)
            state = incoming[g, sub * DV : (sub + 1) * DV, :]
            recur = firsts[sub] + mm(edges[sub], state, ((1,), (1,)))
            scale = lax.rsqrt(jnp.mean(recur * recur, axis=-1, keepdims=True) + 1e-06)
            normed[:, lanes] = (recur * scale * gain_ref[...] * silu(gate_ref[:, lanes])).astype(BF16)
        return carry

    lax.fori_loop(0, heads_k, query_side, 0)

    loads[3].wait()
    tiles = depth // OUT_TILE

    def rows_for(which):
        return jnp.concatenate(
            [
                normed[pl.ds(pl.multiple_of((chip_at(d) * 2 + which) * rows, 16), rows), :]
                for d in range(chips)
            ],
            axis=0,
        )

    def core_copy(t):
        return remote(core_out.at[t], core_in.at[t], core_send.at[t], core_recv.at[t], {"tp": partner})

    def chip_copy(t, d):
        return remote(
            chip_out.at[t, d - 1], chip_in.at[t, d - 1], chip_send.at[t, d - 1], chip_recv.at[t, d - 1], on_chip(d)
        )

    def for_partner(t, carry):
        lanes = pl.ds(pl.multiple_of(t * OUT_TILE, OUT_TILE), OUT_TILE)
        core_out[t] = mm(rows_for(1 - core), w_output[:, lanes]).astype(BF16)
        core_copy(t).start()
        return carry

    lax.fori_loop(0, tiles, for_partner, 0)

    def for_core(t, carry):
        lanes = pl.ds(pl.multiple_of(t * OUT_TILE, OUT_TILE), OUT_TILE)
        part = mm(rows_for(core), w_output[:, lanes])
        core_copy(t).wait_recv()
        part = part + core_in[t].astype(F32)
        for d in range(1, chips):
            chip_out[t, d - 1] = part[d * rows : (d + 1) * rows].astype(BF16)
            chip_copy(t, d).start()
        total[:, lanes] = part[:rows]
        return carry

    lax.fori_loop(0, tiles, for_core, 0)

    def finish(t, carry):
        lanes = pl.ds(pl.multiple_of(t * OUT_TILE, OUT_TILE), OUT_TILE)
        part = total[:, lanes]
        for d in range(1, chips):
            chip_copy(t, d).wait_recv()
            part = part + chip_in[t, d - 1].astype(F32)
        out_ref[:, lanes] = part.astype(BF16)
        return carry

    lax.fori_loop(0, tiles, finish, 0)

    for copy in across + passes:
        copy.wait_send()

    def drain_sums(t, carry):
        core_copy(t).wait_send()
        for d in range(1, chips):
            chip_copy(t, d).wait_send()
        return carry

    lax.fori_loop(0, tiles, drain_sums, 0)

    @pl.when(not_last)
    def _():
        tail_copy.wait_send()

        def drain(g, carry):
            state_copy(g).wait_send()
            return carry

        lax.fori_loop(0, heads_k, drain, 0)


def local(
    devices,
    peers,
    tokens,
    w_query_key,
    w_value,
    w_gate_out,
    conv_query_key,
    conv_value,
    log_decay,
    beta,
    seg_start,
    norm_gain,
    w_output,
):
    width_qk = w_query_key.shape[2]
    width_v = w_value.shape[1]
    heads_k = width_qk // DK
    heads_v = width_v // DV
    count = seg_start.shape[0]
    rows, depth = tokens.shape
    width = 2 * width_qk + width_v
    chips = peers // 2
    others = max(chips - 1, 1)
    tiles = depth // OUT_TILE
    vmem = pl.BlockSpec(memory_space=pltpu.VMEM)
    anywhere = pl.BlockSpec(memory_space=pl.ANY)
    dma = pltpu.SemaphoreType.DMA
    return pl.pallas_call(
        functools.partial(layer, devices, peers, heads_v // heads_k),
        out_shape=jax.ShapeDtypeStruct((rows, depth), BF16),
        in_specs=[vmem] * 7 + [anywhere] * 4,
        out_specs=vmem,
        scratch_shapes=[
            pltpu.VMEM(w_query_key.shape, BF16),
            pltpu.VMEM(w_value.shape, BF16),
            pltpu.VMEM(w_gate_out.shape, BF16),
            pltpu.VMEM(w_output.shape, BF16),
            pltpu.VMEM((count, depth), BF16),
            pltpu.VMEM((TAIL, width), BF16),
            pltpu.VMEM((count, width_v), F32),
            pltpu.VMEM((count, width_v), BF16),
            pltpu.VMEM((TAIL + count, width), F32),
            pltpu.VMEM((TAIL, width), BF16),
            pltpu.VMEM((HALF, HALF), jnp.int32),
            pltpu.VMEM((heads_v, count), F32),
            pltpu.VMEM((count, width_qk), BF16),
            pltpu.VMEM((heads_v, count, count), F32),
            pltpu.VMEM((heads_v, count, DV + DK), BF16),
            pltpu.VMEM((heads_v, DK, DK), BF16),
            pltpu.VMEM((heads_v, DK, DK), BF16),
            pltpu.VMEM((heads_v, DV, DK), F32),
            pltpu.VMEM((heads_k, heads_v // heads_k * DV, DK), BF16),
            pltpu.VMEM((heads_k, heads_v // heads_k * DV, DK), BF16),
            pltpu.VMEM((tiles, chips * rows, OUT_TILE), BF16),
            pltpu.VMEM((tiles, chips * rows, OUT_TILE), BF16),
            pltpu.VMEM((tiles, others, rows, OUT_TILE), BF16),
            pltpu.VMEM((tiles, others, rows, OUT_TILE), BF16),
            pltpu.VMEM((rows, depth), F32),
            dma((4,)),
            dma((2,)),
            dma((heads_k,)),
            dma((heads_k,)),
            dma((chips,)),
            dma((chips,)),
            dma((chips,)),
            dma((chips,)),
            dma((tiles,)),
            dma((tiles,)),
            dma((tiles, others)),
            dma((tiles, others)),
        ],
        compiler_params=pltpu.CompilerParams(
            collective_id=0, has_side_effects=True, vmem_limit_bytes=56 << 20
        ),
    )(
        tokens,
        conv_query_key,
        conv_value,
        log_decay,
        beta,
        seg_start.reshape(1, count),
        norm_gain.reshape(1, DV),
        w_query_key,
        w_value,
        w_gate_out,
        w_output,
    )


def solution(mesh):
    return jax.shard_map(
        functools.partial(local, mesh.shape["ctx"], mesh.shape["tp"]),
        mesh=mesh,
        in_specs=(
            P(("ctx", "tp"), None),
            P(None, None, "tp"),
            P(None, "tp"),
            P(None, "tp"),
            P(None, None, "tp"),
            P(None, "tp"),
            P("tp", "ctx"),
            P("tp", "ctx"),
            P("ctx"),
            P(),
            P("tp", None),
        ),
        out_specs=P(("ctx", "tp"), None),
        check_vma=False,
    )
```

```python
import functools

import jax
import jax.numpy as jnp
from jax import lax
from jax.experimental import pallas as pl
from jax.experimental.pallas import tpu as pltpu
from jax.sharding import PartitionSpec as P

DK = 128
DV = 128
CONV = 4
TAIL = 16
HALF = 128
TILE = 256
OUT_TILE = 512

MESH = pl.DeviceIdType.MESH
F32 = jnp.float32
BF16 = jnp.bfloat16


def mm(a, b, dims=((1,), (0,))):
    return lax.dot_general(a, b, (dims, ((), ())), preferred_element_type=F32)


def halves(a):
    high = a.astype(BF16)
    return high, (a - high.astype(F32)).astype(BF16)


def mm3(a, b):
    a_high, a_low = halves(a)
    b_high, b_low = halves(b)
    return mm(a_high, b_high) + (mm(a_high, b_low) + mm(a_low, b_high))


def column(row):
    return jnp.broadcast_to(row, (8, row.shape[1])).T[:, :1]


def iota(shape, dim):
    return lax.broadcasted_iota(jnp.int32, shape, dim)


def silu(x):
    return x / (1.0 + jnp.exp(-x))


def level_of(size):
    diff = jnp.bitwise_xor(iota((size, size), 0), iota((size, size), 1))
    level = jnp.zeros((size, size), jnp.int32)
    for bit in range(size.bit_length() - 1):
        level = level + (diff >= (1 << bit)).astype(jnp.int32)
    return level


def unit_lower_inverses(lowers, level, eye):
    size = lowers[0].shape[0]
    inverses = [eye - jnp.where(level == 1, lower, 0.0) for lower in lowers]
    for step in range(2, size.bit_length()):
        joints = [jnp.where(level == step, lower, 0.0).astype(BF16) for lower in lowers]
        rounded = [inverse.astype(BF16) for inverse in inverses]
        firsts = [mm(x, joint).astype(BF16) for x, joint in zip(rounded, joints)]
        seconds = [mm(first, x) for first, x in zip(firsts, rounded)]
        inverses = [inverse - second for inverse, second in zip(inverses, seconds)]
    rests = [eye - inverse - mm3(lower, inverse) for lower, inverse in zip(lowers, inverses)]
    return [inverse + mm(inverse.astype(BF16), rest.astype(BF16)) for inverse, rest in zip(inverses, rests)]


def layer(
    devices,
    peers,
    repeat,
    tokens_ref,
    taps_query_key,
    taps_value,
    logd_ref,
    beta_ref,
    seg_ref,
    gain_ref,
    w_query_key_hbm,
    w_value_hbm,
    w_gate_hbm,
    w_output_hbm,
    out_ref,
    w_query_key,
    w_value,
    w_gate,
    w_output,
    gathered,
    tail_out,
    gate_ref,
    normed,
    ext,
    tail,
    level_ref,
    gam_ref,
    keys,
    decays,
    corrected,
    map_high,
    map_low,
    bmat,
    outgoing,
    incoming,
    entering,
    maps_out,
    maps_in,
    leads_out,
    leads_in,
    core_out,
    core_in,
    chip_out,
    chip_in,
    total,
    weight_sems,
    tail_sems,
    send_sems,
    recv_sems,
    far_send,
    maps_send,
    maps_recv,
    leads_send,
    leads_recv,
    gather_send,
    gather_recv,
    pass_send,
    pass_recv,
    core_send,
    core_recv,
    chip_send,
    chip_recv,
):
    me = lax.axis_index("ctx")
    slot = lax.axis_index("tp")
    core, chip, chips = slot % 2, slot // 2, peers // 2
    partner = chip * 2 + 1 - core
    not_first = me > 0
    not_last = me < devices - 1
    pair = me // 2
    odd = me % 2 == 1
    even = me % 2 == 0
    has_before = jnp.logical_and(odd, me > 2)
    has_after = jnp.logical_and(odd, not_last)
    rows, depth = tokens_ref.shape
    count = rows * peers
    heads_v = logd_ref.shape[0]
    heads_k = heads_v // repeat
    width_qk = heads_k * DK
    width_v = heads_v * DV
    width = 2 * width_qk + width_v

    loads = [
        pltpu.make_async_copy(src, dst, weight_sems.at[n])
        for n, (src, dst) in enumerate(
            [
                (w_query_key_hbm, w_query_key),
                (w_value_hbm, w_value),
                (w_gate_hbm, w_gate),
                (w_output_hbm, w_output),
            ]
        )
    ]
    for load in loads:
        load.start()

    def chip_at(d):
        return lax.rem(chip + d, chips)

    def on_chip(d):
        return {"tp": chip_at(d) * 2 + core}

    barrier = pltpu.get_barrier_semaphore()

    @pl.when(not_first)
    def _():
        pl.semaphore_signal(barrier, inc=1, device_id={"ctx": me - 1}, device_id_type=MESH)

    @pl.when(not_last)
    def _():
        pl.semaphore_signal(barrier, inc=1, device_id={"ctx": me + 1}, device_id_type=MESH)

    @pl.when(has_before)
    def _():
        pl.semaphore_signal(barrier, inc=1, device_id={"ctx": me - 2}, device_id_type=MESH)

    @pl.when(has_after)
    def _():
        pl.semaphore_signal(barrier, inc=1, device_id={"ctx": me + 2}, device_id_type=MESH)

    pl.semaphore_signal(barrier, inc=1, device_id={"tp": partner}, device_id_type=MESH)
    for d in range(1, chips):
        pl.semaphore_signal(barrier, inc=1, device_id=on_chip(d), device_id_type=MESH)
    near = not_first.astype(jnp.int32) + not_last.astype(jnp.int32)
    far = has_before.astype(jnp.int32) + has_after.astype(jnp.int32)
    pl.semaphore_wait(barrier, near + far + chips)

    def remote(src, dst, send, recv, device):
        return pltpu.make_async_remote_copy(
            src_ref=src, dst_ref=dst, send_sem=send, recv_sem=recv, device_id=device, device_id_type=MESH
        )

    def block(index):
        return gathered.at[pl.ds(pl.multiple_of(index * rows, 16), rows)]

    across = [
        remote(tokens_ref, block(slot), gather_send.at[d], gather_recv.at[d], on_chip(d))
        for d in range(1, chips)
    ]
    for copy in across:
        copy.start()
    passes = [remote(tokens_ref, block(slot), pass_send.at[0], pass_recv.at[0], {"tp": partner})]
    passes[0].start()
    gathered[pl.ds(pl.multiple_of(slot * rows, 16), rows), :] = tokens_ref[...]

    level_ref[...] = level_of(HALF)
    upper = (iota((count, count), 0) <= iota((count, count), 1)).astype(F32)
    gam_ref[...] = lax.dot_general(
        logd_ref[...], upper, (((1,), (0,)), ((), ())), precision=lax.Precision.HIGHEST,
        preferred_element_type=F32,
    )

    for d in range(1, chips):
        across[d - 1].wait_recv()
        came = chip_at(chips - d) * 2 + core
        passes.append(remote(block(came), block(came), pass_send.at[d], pass_recv.at[d], {"tp": partner}))
        passes[d].start()
    for copy in passes:
        copy.wait_recv()

    def project_pre(weight, first, columns):
        def tile(t, carry):
            lanes = pl.ds(pl.multiple_of(t * TILE, TILE), TILE)
            to = pl.ds(pl.multiple_of(first + t * TILE, TILE), TILE)
            part = mm(gathered[...], weight[:, lanes]).astype(BF16)
            ext[TAIL:, to] = part.astype(F32)
            tail_out[:, to] = part[count - TAIL :]
            return carry

        lax.fori_loop(0, columns // TILE, tile, 0)

    loads[0].wait()
    project_pre(w_query_key.at[0], 0, width_qk)
    project_pre(w_query_key.at[1], width_qk, width_qk)
    loads[1].wait()
    project_pre(w_value, 2 * width_qk, width_v)

    tail_copy = remote(tail_out, tail, tail_sems.at[0], tail_sems.at[1], {"ctx": me + 1})

    @pl.when(not_last)
    def _():
        tail_copy.start()

    loads[2].wait()

    def project_gate(t, carry):
        lanes = pl.ds(pl.multiple_of(t * TILE, TILE), TILE)
        gate_ref[:, lanes] = mm(gathered[...], w_gate[:, lanes])
        return carry

    lax.fori_loop(0, width_v // TILE, project_gate, 0)

    @pl.when(jnp.logical_not(not_first))
    def _():
        ext[:TAIL, :] = jnp.zeros((TAIL, width), F32)

    @pl.when(not_first)
    def _():
        tail_copy.wait_recv()
        ext[:TAIL, :] = tail[...].astype(F32)

    offset = me * count
    seg_row = seg_ref[...].astype(F32)
    seg_col = column(seg_row)
    position = (offset + iota((count, 1), 0)).astype(F32)
    since = position - seg_col
    valids = [(since >= float(CONV - 1 - j)).astype(F32) for j in range(CONV)]
    enters = (seg_col < offset.astype(F32)).astype(F32)
    same_last = seg_col == jnp.max(seg_row, axis=1, keepdims=True)

    def conv(at, taps_ref, tap_at):
        lanes = pl.ds(pl.multiple_of(at, 128), 128)
        tap_lanes = pl.ds(pl.multiple_of(tap_at, 128), 128)
        total = None
        for j in range(CONV):
            term = ext[TAIL - (CONV - 1) + j : TAIL - (CONV - 1) + j + count, lanes] * (
                taps_ref[j : j + 1, tap_lanes] * valids[j]
            )
            total = term if total is None else total + term
        return silu(total)

    def unit(x):
        return x * lax.rsqrt(jnp.sum(x * x, axis=-1, keepdims=True) + 1e-06)

    def to_next(g):
        return remote(outgoing.at[g], incoming.at[g], send_sems.at[g], recv_sems.at[g], {"ctx": me + 1})

    def to_pair(g):
        return remote(outgoing.at[g], incoming.at[g], far_send.at[g], recv_sems.at[g], {"ctx": me + 2})

    def map_copies(g):
        to = {"ctx": me + 1}
        return (
            remote(maps_out.at[g], maps_in.at[g], maps_send.at[g], maps_recv.at[g], to),
            remote(leads_out.at[g], leads_in.at[g], leads_send.at[g], leads_recv.at[g], to),
        )

    def head_lanes(h):
        return pl.ds(pl.multiple_of(h * DV, 128), DV)

    span = DV + DK

    def join_maps(g):
        for copy in map_copies(g):
            copy.wait_recv()
        for sub in range(repeat):
            h = g * repeat + sub
            high, low = map_high[h], map_low[h]
            slab = maps_in[g, sub * span : (sub + 1) * span, :]
            product = mm(slab, high) + mm(slab, low)
            bmat[h] = bmat[h] + product[:DV]
            lead = leads_in[g, sub : sub + 1, :]
            map_high[h], map_low[h] = halves(lead * (high.astype(F32) + low.astype(F32)) - product[DV:])

    def pass_state(g):
        @pl.when(pair > 0)
        def _():
            to_next(g).wait_recv()

        @pl.when(pair == 0)
        def _():
            incoming[g] = jnp.zeros((repeat * DV, DK), BF16)

        @pl.when(has_after)
        def _():
            for sub in range(repeat):
                h = g * repeat + sub
                part = slice(sub * DV, (sub + 1) * DV)
                state = incoming[g, part, :]
                outgoing[g, part, :] = (mm(state, map_high[h]) + mm(state, map_low[h]) + bmat[h]).astype(BF16)
            to_pair(g).start()
            to_next(g).start()

        @pl.when(odd)
        def _():
            for sub in range(repeat):
                part = slice(sub * DV, (sub + 1) * DV)
                state = incoming[g, part, :]
                b_slab = maps_in[g, sub * span : sub * span + DV, :]
                m_slab = maps_in[g, sub * span + DV : (sub + 1) * span, :]
                kept = leads_in[g, sub : sub + 1, :] * state.astype(F32)
                entering[g, part, :] = (kept - mm(state, m_slab) + b_slab.astype(F32)).astype(BF16)

        @pl.when(even)
        def _():
            entering[g] = incoming[g]

    ahead = jnp.minimum(jnp.where(odd, 1 + pair, heads_k), heads_k)
    eye = (iota((HALF, HALF), 0) == iota((HALF, HALF), 1)).astype(F32)
    parts = [slice(b * HALF, (b + 1) * HALF) for b in range(count // HALF)]

    def key_side(g, carry):
        key = unit(conv(width_qk + g * DK, taps_query_key.at[1], g * DK))
        key_b = key.astype(BF16)
        keys[:, head_lanes(g)] = key_b
        keys_dot = mm(key_b, key_b, ((1,), (1,)))
        rows_i, cols_i = iota((count, count), 0), iota((count, count), 1)
        within = jnp.logical_and(rows_i >= cols_i, seg_col == seg_row)
        strict = jnp.logical_and(rows_i > cols_i, within)
        level = level_ref[...]
        lowers, sides, lasts, leads = [], [], [], []
        for sub in range(repeat):
            h = g * repeat + sub
            value = conv(2 * width_qk + h * DV, taps_value, h * DV)
            gam_row = gam_ref[pl.ds(h, 1), :]
            gam_col = column(gam_row)
            beta_col = column(beta_ref[pl.ds(h, 1), :])
            decay = jnp.where(within, jnp.exp(jnp.where(within, gam_col - gam_row, 0.0)), 0.0)
            decays[h] = decay
            lead = jnp.exp(gam_col) * enters
            lowers.append(jnp.where(strict, beta_col * keys_dot * decay, 0.0))
            sides.append(jnp.concatenate([beta_col * value, (beta_col * lead) * key], axis=1))
            gam_last = gam_row[:, count - 1 :]
            lasts.append(jnp.where(same_last, jnp.exp(jnp.where(same_last, gam_last - gam_col, 0.0)), 0.0))
            leads.append(lead[count - 1 :, :])
        inverses = unit_lower_inverses([lower[r, r] for lower in lowers for r in parts], level, eye)
        solved = [[] for _ in range(repeat)]
        for b, r in enumerate(parts):
            for sub in range(repeat):
                part = sides[sub][r]
                if b:
                    part = part - mm3(lowers[sub][r, : b * HALF], jnp.concatenate(solved[sub], axis=0))
                solved[sub].append(mm3(inverses[sub * len(parts) + b], part))
        for sub in range(repeat):
            h = g * repeat + sub
            w_both = jnp.concatenate(solved[sub], axis=0)
            corrected[h] = w_both.astype(BF16)
            maps = mm((w_both * lasts[sub]).astype(BF16), key_b, ((0,), (0,)))
            bmat[h] = maps[:DV]
            map_high[h], map_low[h] = halves(leads[sub] * eye - maps[DV:])
            maps_out[g, sub * span : (sub + 1) * span, :] = maps.astype(BF16)
            leads_out[g, sub : sub + 1, :] = jnp.broadcast_to(leads[sub], (1, DK))

        @pl.when(even)
        def _():
            for copy in map_copies(g):
                copy.start()

        @pl.when(jnp.logical_and(odd, g >= 1))
        def _():
            join_maps(g - 1)

        @pl.when(g >= ahead)
        def _():
            pass_state(g - ahead)

        return carry

    lax.fori_loop(0, heads_k, key_side, 0)

    @pl.when(odd)
    def _():
        join_maps(heads_k - 1)

    def query_side(g, carry):
        query = unit(conv(g * DK, taps_query_key.at[0], g * DK)) * DK ** (-0.5)
        query_dot = mm(query.astype(BF16), keys[:, head_lanes(g)], ((1,), (1,)))
        firsts, edges = [], []
        for sub in range(repeat):
            h = g * repeat + sub
            lead = jnp.exp(column(gam_ref[pl.ds(h, 1), :])) * enters
            both = mm((query_dot * decays[h]).astype(BF16), corrected[h])
            firsts.append(both[:, :DV])
            edges.append((lead * query - both[:, DV:]).astype(BF16))

        @pl.when(g >= heads_k - ahead)
        def _():
            pass_state(g)

        for sub in range(repeat):
            lanes = head_lanes(g * repeat + sub)
            state = entering[g, sub * DV : (sub + 1) * DV, :]
            recur = firsts[sub] + mm(edges[sub], state, ((1,), (1,)))
            scale = lax.rsqrt(jnp.mean(recur * recur, axis=-1, keepdims=True) + 1e-06)
            normed[:, lanes] = (recur * scale * gain_ref[...] * silu(gate_ref[:, lanes])).astype(BF16)
        return carry

    lax.fori_loop(0, heads_k, query_side, 0)

    loads[3].wait()
    tiles = depth // OUT_TILE

    def rows_for(which):
        return jnp.concatenate(
            [
                normed[pl.ds(pl.multiple_of((chip_at(d) * 2 + which) * rows, 16), rows), :]
                for d in range(chips)
            ],
            axis=0,
        )

    def core_copy(t):
        return remote(core_out.at[t], core_in.at[t], core_send.at[t], core_recv.at[t], {"tp": partner})

    def chip_copy(t, d):
        return remote(
            chip_out.at[t, d - 1], chip_in.at[t, d - 1], chip_send.at[t, d - 1], chip_recv.at[t, d - 1], on_chip(d)
        )

    def for_partner(t, carry):
        lanes = pl.ds(pl.multiple_of(t * OUT_TILE, OUT_TILE), OUT_TILE)
        core_out[t] = mm(rows_for(1 - core), w_output[:, lanes]).astype(BF16)
        core_copy(t).start()
        return carry

    lax.fori_loop(0, tiles, for_partner, 0)

    def for_core(t, carry):
        lanes = pl.ds(pl.multiple_of(t * OUT_TILE, OUT_TILE), OUT_TILE)
        part = mm(rows_for(core), w_output[:, lanes])
        core_copy(t).wait_recv()
        part = part + core_in[t].astype(F32)
        for d in range(1, chips):
            chip_out[t, d - 1] = part[d * rows : (d + 1) * rows].astype(BF16)
            chip_copy(t, d).start()
        total[:, lanes] = part[:rows]
        return carry

    lax.fori_loop(0, tiles, for_core, 0)

    def finish(t, carry):
        lanes = pl.ds(pl.multiple_of(t * OUT_TILE, OUT_TILE), OUT_TILE)
        part = total[:, lanes]
        for d in range(1, chips):
            chip_copy(t, d).wait_recv()
            part = part + chip_in[t, d - 1].astype(F32)
        out_ref[:, lanes] = part.astype(BF16)
        return carry

    lax.fori_loop(0, tiles, finish, 0)

    for copy in across + passes:
        copy.wait_send()

    def drain_sums(t, carry):
        core_copy(t).wait_send()
        for d in range(1, chips):
            chip_copy(t, d).wait_send()
        return carry

    lax.fori_loop(0, tiles, drain_sums, 0)

    @pl.when(not_last)
    def _():
        tail_copy.wait_send()

    @pl.when(has_after)
    def _():
        def drain(g, carry):
            to_pair(g).wait_send()
            to_next(g).wait_send()
            return carry

        lax.fori_loop(0, heads_k, drain, 0)

    @pl.when(even)
    def _():
        def drain(g, carry):
            for copy in map_copies(g):
                copy.wait_send()
            return carry

        lax.fori_loop(0, heads_k, drain, 0)


def local(
    devices,
    peers,
    tokens,
    w_query_key,
    w_value,
    w_gate_out,
    conv_query_key,
    conv_value,
    log_decay,
    beta,
    seg_start,
    norm_gain,
    w_output,
):
    width_qk = w_query_key.shape[2]
    width_v = w_value.shape[1]
    heads_k = width_qk // DK
    heads_v = width_v // DV
    count = seg_start.shape[0]
    rows, depth = tokens.shape
    width = 2 * width_qk + width_v
    chips = peers // 2
    others = max(chips - 1, 1)
    tiles = depth // OUT_TILE
    vmem = pl.BlockSpec(memory_space=pltpu.VMEM)
    anywhere = pl.BlockSpec(memory_space=pl.ANY)
    dma = pltpu.SemaphoreType.DMA
    return pl.pallas_call(
        functools.partial(layer, devices, peers, heads_v // heads_k),
        out_shape=jax.ShapeDtypeStruct((rows, depth), BF16),
        in_specs=[vmem] * 7 + [anywhere] * 4,
        out_specs=vmem,
        scratch_shapes=[
            pltpu.VMEM(w_query_key.shape, BF16),
            pltpu.VMEM(w_value.shape, BF16),
            pltpu.VMEM(w_gate_out.shape, BF16),
            pltpu.VMEM(w_output.shape, BF16),
            pltpu.VMEM((count, depth), BF16),
            pltpu.VMEM((TAIL, width), BF16),
            pltpu.VMEM((count, width_v), F32),
            pltpu.VMEM((count, width_v), BF16),
            pltpu.VMEM((TAIL + count, width), F32),
            pltpu.VMEM((TAIL, width), BF16),
            pltpu.VMEM((HALF, HALF), jnp.int32),
            pltpu.VMEM((heads_v, count), F32),
            pltpu.VMEM((count, width_qk), BF16),
            pltpu.VMEM((heads_v, count, count), F32),
            pltpu.VMEM((heads_v, count, DV + DK), BF16),
            pltpu.VMEM((heads_v, DK, DK), BF16),
            pltpu.VMEM((heads_v, DK, DK), BF16),
            pltpu.VMEM((heads_v, DV, DK), F32),
            pltpu.VMEM((heads_k, heads_v // heads_k * DV, DK), BF16),
            pltpu.VMEM((heads_k, heads_v // heads_k * DV, DK), BF16),
            pltpu.VMEM((heads_k, heads_v // heads_k * DV, DK), BF16),
            pltpu.VMEM((heads_k, heads_v // heads_k * (DV + DK), DK), BF16),
            pltpu.VMEM((heads_k, heads_v // heads_k * (DV + DK), DK), BF16),
            pltpu.VMEM((heads_k, 8, DK), F32),
            pltpu.VMEM((heads_k, 8, DK), F32),
            pltpu.VMEM((tiles, chips * rows, OUT_TILE), BF16),
            pltpu.VMEM((tiles, chips * rows, OUT_TILE), BF16),
            pltpu.VMEM((tiles, others, rows, OUT_TILE), BF16),
            pltpu.VMEM((tiles, others, rows, OUT_TILE), BF16),
            pltpu.VMEM((rows, depth), F32),
            dma((4,)),
            dma((2,)),
            dma((heads_k,)),
            dma((heads_k,)),
            dma((heads_k,)),
            dma((heads_k,)),
            dma((heads_k,)),
            dma((heads_k,)),
            dma((heads_k,)),
            dma((chips,)),
            dma((chips,)),
            dma((chips,)),
            dma((chips,)),
            dma((tiles,)),
            dma((tiles,)),
            dma((tiles, others)),
            dma((tiles, others)),
        ],
        compiler_params=pltpu.CompilerParams(
            collective_id=0, has_side_effects=True, vmem_limit_bytes=56 << 20
        ),
    )(
        tokens,
        conv_query_key,
        conv_value,
        log_decay,
        beta,
        seg_start.reshape(1, count),
        norm_gain.reshape(1, DV),
        w_query_key,
        w_value,
        w_gate_out,
        w_output,
    )


def solution(mesh):
    return jax.shard_map(
        functools.partial(local, mesh.shape["ctx"], mesh.shape["tp"]),
        mesh=mesh,
        in_specs=(
            P(("ctx", "tp"), None),
            P(None, None, "tp"),
            P(None, "tp"),
            P(None, "tp"),
            P(None, None, "tp"),
            P(None, "tp"),
            P("tp", "ctx"),
            P("tp", "ctx"),
            P("ctx"),
            P(),
            P("tp", None),
        ),
        out_specs=P(("ctx", "tp"), None),
        check_vma=False,
    )
```

```python
import functools

import jax
import jax.numpy as jnp
from jax import lax
from jax.experimental import pallas as pl
from jax.experimental.pallas import tpu as pltpu
from jax.sharding import PartitionSpec as P

DK = 128
DV = 128
CONV = 4
TAIL = 16
HALF = 128
TILE = 256
OUT_TILE = 512

MESH = pl.DeviceIdType.MESH
F32 = jnp.float32
BF16 = jnp.bfloat16


def mm(a, b, dims=((1,), (0,))):
    return lax.dot_general(a, b, (dims, ((), ())), preferred_element_type=F32)


def halves(a):
    high = a.astype(BF16)
    return high, (a - high.astype(F32)).astype(BF16)


def mm3(a, b):
    a_high, a_low = halves(a)
    b_high, b_low = halves(b)
    return mm(a_high, b_high) + (mm(a_high, b_low) + mm(a_low, b_high))


def column(row):
    return jnp.broadcast_to(row, (8, row.shape[1])).T[:, :1]


def iota(shape, dim):
    return lax.broadcasted_iota(jnp.int32, shape, dim)


def silu(x):
    return x / (1.0 + jnp.exp(-x))


def level_of(size):
    diff = jnp.bitwise_xor(iota((size, size), 0), iota((size, size), 1))
    level = jnp.zeros((size, size), jnp.int32)
    for bit in range(size.bit_length() - 1):
        level = level + (diff >= (1 << bit)).astype(jnp.int32)
    return level


def unit_lower_inverses(lowers, level, eye):
    size = lowers[0].shape[0]
    inverses = [eye - jnp.where(level == 1, lower, 0.0) for lower in lowers]
    for step in range(2, size.bit_length()):
        joints = [jnp.where(level == step, lower, 0.0).astype(BF16) for lower in lowers]
        rounded = [inverse.astype(BF16) for inverse in inverses]
        firsts = [mm(x, joint).astype(BF16) for x, joint in zip(rounded, joints)]
        seconds = [mm(first, x) for first, x in zip(firsts, rounded)]
        inverses = [inverse - second for inverse, second in zip(inverses, seconds)]
    rests = [eye - inverse - mm3(lower, inverse) for lower, inverse in zip(lowers, inverses)]
    return [inverse + mm(inverse.astype(BF16), rest.astype(BF16)) for inverse, rest in zip(inverses, rests)]


def layer(
    devices,
    peers,
    repeat,
    tokens_ref,
    taps_query_key,
    taps_value,
    logd_ref,
    beta_ref,
    seg_ref,
    gain_ref,
    w_query_key_hbm,
    w_value_hbm,
    w_gate_hbm,
    w_output_hbm,
    out_ref,
    w_query_key,
    w_value,
    w_gate,
    w_output,
    gathered,
    tail_out,
    gate_ref,
    normed,
    ext,
    tail,
    level_ref,
    gam_ref,
    keys,
    decays,
    corrected,
    map_high,
    map_low,
    bmat,
    outgoing,
    incoming,
    entering,
    maps_out,
    maps_in,
    leads_out,
    leads_in,
    core_out,
    core_in,
    chip_out,
    chip_in,
    total,
    weight_sems,
    tail_sems,
    send_sems,
    recv_sems,
    far_send,
    maps_send,
    maps_recv,
    leads_send,
    leads_recv,
    gather_send,
    gather_recv,
    pass_send,
    pass_recv,
    core_send,
    core_recv,
    chip_send,
    chip_recv,
):
    me = lax.axis_index("ctx")
    slot = lax.axis_index("tp")
    core, chip, chips = slot % 2, slot // 2, peers // 2
    partner = chip * 2 + 1 - core
    not_first = me > 0
    not_last = me < devices - 1
    pair = me // 2
    odd = me % 2 == 1
    even = me % 2 == 0
    has_before = jnp.logical_and(odd, me > 2)
    forwards = jnp.logical_and(odd, pair > 0)
    opens = jnp.logical_and(odd, pair == 0)
    has_after = jnp.logical_and(odd, not_last)
    rows, depth = tokens_ref.shape
    count = rows * peers
    heads_v = logd_ref.shape[0]
    heads_k = heads_v // repeat
    width_qk = heads_k * DK
    width_v = heads_v * DV
    width = 2 * width_qk + width_v

    loads = [
        pltpu.make_async_copy(src, dst, weight_sems.at[n])
        for n, (src, dst) in enumerate(
            [
                (w_query_key_hbm, w_query_key),
                (w_value_hbm, w_value),
                (w_gate_hbm, w_gate),
                (w_output_hbm, w_output),
            ]
        )
    ]
    for load in loads:
        load.start()

    def chip_at(d):
        return lax.rem(chip + d, chips)

    def on_chip(d):
        return {"tp": chip_at(d) * 2 + core}

    barrier = pltpu.get_barrier_semaphore()

    @pl.when(not_first)
    def _():
        pl.semaphore_signal(barrier, inc=1, device_id={"ctx": me - 1}, device_id_type=MESH)

    @pl.when(not_last)
    def _():
        pl.semaphore_signal(barrier, inc=1, device_id={"ctx": me + 1}, device_id_type=MESH)

    @pl.when(has_before)
    def _():
        pl.semaphore_signal(barrier, inc=1, device_id={"ctx": me - 2}, device_id_type=MESH)

    @pl.when(has_after)
    def _():
        pl.semaphore_signal(barrier, inc=1, device_id={"ctx": me + 2}, device_id_type=MESH)

    pl.semaphore_signal(barrier, inc=1, device_id={"tp": partner}, device_id_type=MESH)
    for d in range(1, chips):
        pl.semaphore_signal(barrier, inc=1, device_id=on_chip(d), device_id_type=MESH)
    near = not_first.astype(jnp.int32) + not_last.astype(jnp.int32)
    far = has_before.astype(jnp.int32) + has_after.astype(jnp.int32)
    pl.semaphore_wait(barrier, near + far + chips)

    def remote(src, dst, send, recv, device):
        return pltpu.make_async_remote_copy(
            src_ref=src, dst_ref=dst, send_sem=send, recv_sem=recv, device_id=device, device_id_type=MESH
        )

    def block(index):
        return gathered.at[pl.ds(pl.multiple_of(index * rows, 16), rows)]

    across = [
        remote(tokens_ref, block(slot), gather_send.at[d], gather_recv.at[d], on_chip(d))
        for d in range(1, chips)
    ]
    for copy in across:
        copy.start()
    passes = [remote(tokens_ref, block(slot), pass_send.at[0], pass_recv.at[0], {"tp": partner})]
    passes[0].start()
    gathered[pl.ds(pl.multiple_of(slot * rows, 16), rows), :] = tokens_ref[...]

    level_ref[...] = level_of(HALF)
    upper = (iota((count, count), 0) <= iota((count, count), 1)).astype(F32)
    gam_ref[...] = lax.dot_general(
        logd_ref[...], upper, (((1,), (0,)), ((), ())), precision=lax.Precision.HIGHEST,
        preferred_element_type=F32,
    )

    for d in range(1, chips):
        across[d - 1].wait_recv()
        came = chip_at(chips - d) * 2 + core
        passes.append(remote(block(came), block(came), pass_send.at[d], pass_recv.at[d], {"tp": partner}))
        passes[d].start()
    for copy in passes:
        copy.wait_recv()

    def project_pre(weight, first, columns):
        def tile(t, carry):
            lanes = pl.ds(pl.multiple_of(t * TILE, TILE), TILE)
            to = pl.ds(pl.multiple_of(first + t * TILE, TILE), TILE)
            part = mm(gathered[...], weight[:, lanes]).astype(BF16)
            ext[TAIL:, to] = part.astype(F32)
            tail_out[:, to] = part[count - TAIL :]
            return carry

        lax.fori_loop(0, columns // TILE, tile, 0)

    loads[0].wait()
    project_pre(w_query_key.at[0], 0, width_qk)
    project_pre(w_query_key.at[1], width_qk, width_qk)
    loads[1].wait()
    project_pre(w_value, 2 * width_qk, width_v)

    tail_copy = remote(tail_out, tail, tail_sems.at[0], tail_sems.at[1], {"ctx": me + 1})

    @pl.when(not_last)
    def _():
        tail_copy.start()

    loads[2].wait()

    def project_gate(t, carry):
        lanes = pl.ds(pl.multiple_of(t * TILE, TILE), TILE)
        gate_ref[:, lanes] = mm(gathered[...], w_gate[:, lanes])
        return carry

    lax.fori_loop(0, width_v // TILE, project_gate, 0)

    @pl.when(jnp.logical_not(not_first))
    def _():
        ext[:TAIL, :] = jnp.zeros((TAIL, width), F32)

    @pl.when(not_first)
    def _():
        tail_copy.wait_recv()
        ext[:TAIL, :] = tail[...].astype(F32)

    offset = me * count
    seg_row = seg_ref[...].astype(F32)
    seg_col = column(seg_row)
    position = (offset + iota((count, 1), 0)).astype(F32)
    since = position - seg_col
    valids = [(since >= float(CONV - 1 - j)).astype(F32) for j in range(CONV)]
    enters = (seg_col < offset.astype(F32)).astype(F32)
    same_last = seg_col == jnp.max(seg_row, axis=1, keepdims=True)

    def conv(at, taps_ref, tap_at):
        lanes = pl.ds(pl.multiple_of(at, 128), 128)
        tap_lanes = pl.ds(pl.multiple_of(tap_at, 128), 128)
        total = None
        for j in range(CONV):
            term = ext[TAIL - (CONV - 1) + j : TAIL - (CONV - 1) + j + count, lanes] * (
                taps_ref[j : j + 1, tap_lanes] * valids[j]
            )
            total = term if total is None else total + term
        return silu(total)

    def unit(x):
        return x * lax.rsqrt(jnp.sum(x * x, axis=-1, keepdims=True) + 1e-06)

    def to_even(g):
        return remote(incoming.at[g], incoming.at[g], send_sems.at[g], recv_sems.at[g], {"ctx": me - 1})

    def to_pair(g):
        return remote(outgoing.at[g], incoming.at[g], far_send.at[g], recv_sems.at[g], {"ctx": me + 2})

    def map_copies(g):
        to = {"ctx": me + 1}
        return (
            remote(maps_out.at[g], maps_in.at[g], maps_send.at[g], maps_recv.at[g], to),
            remote(leads_out.at[g], leads_in.at[g], leads_send.at[g], leads_recv.at[g], to),
        )

    def head_lanes(h):
        return pl.ds(pl.multiple_of(h * DV, 128), DV)

    span = DV + DK

    def join_maps(g):
        for copy in map_copies(g):
            copy.wait_recv()
        for sub in range(repeat):
            h = g * repeat + sub
            high, low = map_high[h], map_low[h]
            slab = maps_in[g, sub * span : (sub + 1) * span, :]
            product = mm(slab, high) + mm(slab, low)
            bmat[h] = bmat[h] + product[:DV]
            lead = leads_in[g, sub : sub + 1, :]
            map_high[h], map_low[h] = halves(lead * (high.astype(F32) + low.astype(F32)) - product[DV:])

    def pass_state(g):
        @pl.when(pair > 0)
        def _():
            to_pair(g).wait_recv()

        @pl.when(forwards)
        def _():
            to_even(g).start()

        @pl.when(pair == 0)
        def _():
            incoming[g] = jnp.zeros((repeat * DV, DK), BF16)

        @pl.when(has_after)
        def _():
            for sub in range(repeat):
                h = g * repeat + sub
                part = slice(sub * DV, (sub + 1) * DV)
                state = incoming[g, part, :]
                outgoing[g, part, :] = (mm(state, map_high[h]) + mm(state, map_low[h]) + bmat[h]).astype(BF16)
            to_pair(g).start()

        @pl.when(odd)
        def _():
            for sub in range(repeat):
                part = slice(sub * DV, (sub + 1) * DV)
                state = incoming[g, part, :]
                b_slab = maps_in[g, sub * span : sub * span + DV, :]
                m_slab = maps_in[g, sub * span + DV : (sub + 1) * span, :]
                kept = leads_in[g, sub : sub + 1, :] * state.astype(F32)
                entering[g, part, :] = (kept - mm(state, m_slab) + b_slab.astype(F32)).astype(BF16)

        @pl.when(even)
        def _():
            entering[g] = incoming[g]

    ahead = jnp.minimum(jnp.where(odd, 1 + pair, heads_k), heads_k)
    eye = (iota((HALF, HALF), 0) == iota((HALF, HALF), 1)).astype(F32)
    parts = [slice(b * HALF, (b + 1) * HALF) for b in range(count // HALF)]

    def key_side(g, carry):
        key = unit(conv(width_qk + g * DK, taps_query_key.at[1], g * DK))
        key_b = key.astype(BF16)
        keys[:, head_lanes(g)] = key_b
        keys_dot = mm(key_b, key_b, ((1,), (1,)))
        rows_i, cols_i = iota((count, count), 0), iota((count, count), 1)
        within = jnp.logical_and(rows_i >= cols_i, seg_col == seg_row)
        strict = jnp.logical_and(rows_i > cols_i, within)
        level = level_ref[...]
        lowers, sides, lasts, leads = [], [], [], []
        for sub in range(repeat):
            h = g * repeat + sub
            value = conv(2 * width_qk + h * DV, taps_value, h * DV)
            gam_row = gam_ref[pl.ds(h, 1), :]
            gam_col = column(gam_row)
            beta_col = column(beta_ref[pl.ds(h, 1), :])
            decay = jnp.where(within, jnp.exp(jnp.where(within, gam_col - gam_row, 0.0)), 0.0)
            decays[h] = decay
            lead = jnp.exp(gam_col) * enters
            lowers.append(jnp.where(strict, beta_col * keys_dot * decay, 0.0))
            sides.append(jnp.concatenate([beta_col * value, (beta_col * lead) * key], axis=1))
            gam_last = gam_row[:, count - 1 :]
            lasts.append(jnp.where(same_last, jnp.exp(jnp.where(same_last, gam_last - gam_col, 0.0)), 0.0))
            leads.append(lead[count - 1 :, :])
        inverses = unit_lower_inverses([lower[r, r] for lower in lowers for r in parts], level, eye)
        solved = [[] for _ in range(repeat)]
        for b, r in enumerate(parts):
            for sub in range(repeat):
                part = sides[sub][r]
                if b:
                    part = part - mm3(lowers[sub][r, : b * HALF], jnp.concatenate(solved[sub], axis=0))
                solved[sub].append(mm3(inverses[sub * len(parts) + b], part))
        for sub in range(repeat):
            h = g * repeat + sub
            w_both = jnp.concatenate(solved[sub], axis=0)
            corrected[h] = w_both.astype(BF16)
            maps = mm((w_both * lasts[sub]).astype(BF16), key_b, ((0,), (0,)))
            bmat[h] = maps[:DV]
            map_high[h], map_low[h] = halves(leads[sub] * eye - maps[DV:])
            maps_out[g, sub * span : (sub + 1) * span, :] = maps.astype(BF16)
            leads_out[g, sub : sub + 1, :] = jnp.broadcast_to(leads[sub], (1, DK))

        @pl.when(even)
        def _():
            for copy in map_copies(g):
                copy.start()

        @pl.when(jnp.logical_and(odd, g >= 1))
        def _():
            join_maps(g - 1)

        @pl.when(g >= ahead)
        def _():
            pass_state(g - ahead)

        return carry

    lax.fori_loop(0, heads_k, key_side, 0)

    @pl.when(odd)
    def _():
        join_maps(heads_k - 1)

    @pl.when(opens)
    def _():
        pass_state(heads_k - 1)

    def query_side(g, carry):
        query = unit(conv(g * DK, taps_query_key.at[0], g * DK)) * DK ** (-0.5)
        query_dot = mm(query.astype(BF16), keys[:, head_lanes(g)], ((1,), (1,)))
        firsts, edges = [], []
        for sub in range(repeat):
            h = g * repeat + sub
            lead = jnp.exp(column(gam_ref[pl.ds(h, 1), :])) * enters
            both = mm((query_dot * decays[h]).astype(BF16), corrected[h])
            firsts.append(both[:, :DV])
            edges.append((lead * query - both[:, DV:]).astype(BF16))

        @pl.when(jnp.logical_and(g < ahead, jnp.logical_not(opens)))
        def _():
            pass_state(heads_k - ahead + g)

        for sub in range(repeat):
            lanes = head_lanes(g * repeat + sub)
            state = entering[g, sub * DV : (sub + 1) * DV, :]
            recur = firsts[sub] + mm(edges[sub], state, ((1,), (1,)))
            scale = lax.rsqrt(jnp.mean(recur * recur, axis=-1, keepdims=True) + 1e-06)
            normed[:, lanes] = (recur * scale * gain_ref[...] * silu(gate_ref[:, lanes])).astype(BF16)
        return carry

    lax.fori_loop(0, heads_k, query_side, 0)

    loads[3].wait()
    tiles = depth // OUT_TILE

    def rows_for(which):
        return jnp.concatenate(
            [
                normed[pl.ds(pl.multiple_of((chip_at(d) * 2 + which) * rows, 16), rows), :]
                for d in range(chips)
            ],
            axis=0,
        )

    def core_copy(t):
        return remote(core_out.at[t], core_in.at[t], core_send.at[t], core_recv.at[t], {"tp": partner})

    def chip_copy(t, d):
        return remote(
            chip_out.at[t, d - 1], chip_in.at[t, d - 1], chip_send.at[t, d - 1], chip_recv.at[t, d - 1], on_chip(d)
        )

    def for_partner(t, carry):
        lanes = pl.ds(pl.multiple_of(t * OUT_TILE, OUT_TILE), OUT_TILE)
        core_out[t] = mm(rows_for(1 - core), w_output[:, lanes]).astype(BF16)
        core_copy(t).start()
        return carry

    lax.fori_loop(0, tiles, for_partner, 0)

    def for_core(t, carry):
        lanes = pl.ds(pl.multiple_of(t * OUT_TILE, OUT_TILE), OUT_TILE)
        part = mm(rows_for(core), w_output[:, lanes])
        core_copy(t).wait_recv()
        part = part + core_in[t].astype(F32)
        for d in range(1, chips):
            chip_out[t, d - 1] = part[d * rows : (d + 1) * rows].astype(BF16)
            chip_copy(t, d).start()
        total[:, lanes] = part[:rows]
        return carry

    lax.fori_loop(0, tiles, for_core, 0)

    def finish(t, carry):
        lanes = pl.ds(pl.multiple_of(t * OUT_TILE, OUT_TILE), OUT_TILE)
        part = total[:, lanes]
        for d in range(1, chips):
            chip_copy(t, d).wait_recv()
            part = part + chip_in[t, d - 1].astype(F32)
        out_ref[:, lanes] = part.astype(BF16)
        return carry

    lax.fori_loop(0, tiles, finish, 0)

    for copy in across + passes:
        copy.wait_send()

    def drain_sums(t, carry):
        core_copy(t).wait_send()
        for d in range(1, chips):
            chip_copy(t, d).wait_send()
        return carry

    lax.fori_loop(0, tiles, drain_sums, 0)

    @pl.when(not_last)
    def _():
        tail_copy.wait_send()

    @pl.when(has_after)
    def _():
        def drain(g, carry):
            to_pair(g).wait_send()
            return carry

        lax.fori_loop(0, heads_k, drain, 0)

    @pl.when(forwards)
    def _():
        def drain(g, carry):
            to_even(g).wait_send()
            return carry

        lax.fori_loop(0, heads_k, drain, 0)

    @pl.when(even)
    def _():
        def drain(g, carry):
            for copy in map_copies(g):
                copy.wait_send()
            return carry

        lax.fori_loop(0, heads_k, drain, 0)


def local(
    devices,
    peers,
    tokens,
    w_query_key,
    w_value,
    w_gate_out,
    conv_query_key,
    conv_value,
    log_decay,
    beta,
    seg_start,
    norm_gain,
    w_output,
):
    width_qk = w_query_key.shape[2]
    width_v = w_value.shape[1]
    heads_k = width_qk // DK
    heads_v = width_v // DV
    count = seg_start.shape[0]
    rows, depth = tokens.shape
    width = 2 * width_qk + width_v
    chips = peers // 2
    others = max(chips - 1, 1)
    tiles = depth // OUT_TILE
    vmem = pl.BlockSpec(memory_space=pltpu.VMEM)
    anywhere = pl.BlockSpec(memory_space=pl.ANY)
    dma = pltpu.SemaphoreType.DMA
    return pl.pallas_call(
        functools.partial(layer, devices, peers, heads_v // heads_k),
        out_shape=jax.ShapeDtypeStruct((rows, depth), BF16),
        in_specs=[vmem] * 7 + [anywhere] * 4,
        out_specs=vmem,
        scratch_shapes=[
            pltpu.VMEM(w_query_key.shape, BF16),
            pltpu.VMEM(w_value.shape, BF16),
            pltpu.VMEM(w_gate_out.shape, BF16),
            pltpu.VMEM(w_output.shape, BF16),
            pltpu.VMEM((count, depth), BF16),
            pltpu.VMEM((TAIL, width), BF16),
            pltpu.VMEM((count, width_v), F32),
            pltpu.VMEM((count, width_v), BF16),
            pltpu.VMEM((TAIL + count, width), F32),
            pltpu.VMEM((TAIL, width), BF16),
            pltpu.VMEM((HALF, HALF), jnp.int32),
            pltpu.VMEM((heads_v, count), F32),
            pltpu.VMEM((count, width_qk), BF16),
            pltpu.VMEM((heads_v, count, count), F32),
            pltpu.VMEM((heads_v, count, DV + DK), BF16),
            pltpu.VMEM((heads_v, DK, DK), BF16),
            pltpu.VMEM((heads_v, DK, DK), BF16),
            pltpu.VMEM((heads_v, DV, DK), F32),
            pltpu.VMEM((heads_k, heads_v // heads_k * DV, DK), BF16),
            pltpu.VMEM((heads_k, heads_v // heads_k * DV, DK), BF16),
            pltpu.VMEM((heads_k, heads_v // heads_k * DV, DK), BF16),
            pltpu.VMEM((heads_k, heads_v // heads_k * (DV + DK), DK), BF16),
            pltpu.VMEM((heads_k, heads_v // heads_k * (DV + DK), DK), BF16),
            pltpu.VMEM((heads_k, 8, DK), F32),
            pltpu.VMEM((heads_k, 8, DK), F32),
            pltpu.VMEM((tiles, chips * rows, OUT_TILE), BF16),
            pltpu.VMEM((tiles, chips * rows, OUT_TILE), BF16),
            pltpu.VMEM((tiles, others, rows, OUT_TILE), BF16),
            pltpu.VMEM((tiles, others, rows, OUT_TILE), BF16),
            pltpu.VMEM((rows, depth), F32),
            dma((4,)),
            dma((2,)),
            dma((heads_k,)),
            dma((heads_k,)),
            dma((heads_k,)),
            dma((heads_k,)),
            dma((heads_k,)),
            dma((heads_k,)),
            dma((heads_k,)),
            dma((chips,)),
            dma((chips,)),
            dma((chips,)),
            dma((chips,)),
            dma((tiles,)),
            dma((tiles,)),
            dma((tiles, others)),
            dma((tiles, others)),
        ],
        compiler_params=pltpu.CompilerParams(
            collective_id=0, has_side_effects=True, vmem_limit_bytes=56 << 20
        ),
    )(
        tokens,
        conv_query_key,
        conv_value,
        log_decay,
        beta,
        seg_start.reshape(1, count),
        norm_gain.reshape(1, DV),
        w_query_key,
        w_value,
        w_gate_out,
        w_output,
    )


def solution(mesh):
    return jax.shard_map(
        functools.partial(local, mesh.shape["ctx"], mesh.shape["tp"]),
        mesh=mesh,
        in_specs=(
            P(("ctx", "tp"), None),
            P(None, None, "tp"),
            P(None, "tp"),
            P(None, "tp"),
            P(None, None, "tp"),
            P(None, "tp"),
            P("tp", "ctx"),
            P("tp", "ctx"),
            P("ctx"),
            P(),
            P("tp", None),
        ),
        out_specs=P(("ctx", "tp"), None),
        check_vma=False,
    )
```

```python
import functools

import jax
import jax.numpy as jnp
from jax import lax
from jax.experimental import pallas as pl
from jax.experimental.pallas import tpu as pltpu
from jax.sharding import PartitionSpec as P

DK = 128
DV = 128
CONV = 4
TAIL = 16
HALF = 128
TILE = 256
OUT_TILE = 512

MESH = pl.DeviceIdType.MESH
F32 = jnp.float32
BF16 = jnp.bfloat16


def mm(a, b, dims=((1,), (0,))):
    return lax.dot_general(a, b, (dims, ((), ())), preferred_element_type=F32)


def halves(a):
    high = a.astype(BF16)
    return high, (a - high.astype(F32)).astype(BF16)


def mm3(a, b):
    a_high, a_low = halves(a)
    b_high, b_low = halves(b)
    return mm(a_high, b_high) + (mm(a_high, b_low) + mm(a_low, b_high))


def column(row):
    return jnp.broadcast_to(row, (8, row.shape[1])).T[:, :1]


def iota(shape, dim):
    return lax.broadcasted_iota(jnp.int32, shape, dim)


def silu(x):
    return x / (1.0 + jnp.exp(-x))


def level_of(size):
    diff = jnp.bitwise_xor(iota((size, size), 0), iota((size, size), 1))
    level = jnp.zeros((size, size), jnp.int32)
    for bit in range(size.bit_length() - 1):
        level = level + (diff >= (1 << bit)).astype(jnp.int32)
    return level


def unit_lower_inverses(lowers, level, eye):
    size = lowers[0].shape[0]
    inverses = [eye - jnp.where(level == 1, lower, 0.0) for lower in lowers]
    for step in range(2, size.bit_length()):
        joints = [jnp.where(level == step, lower, 0.0).astype(BF16) for lower in lowers]
        rounded = [inverse.astype(BF16) for inverse in inverses]
        firsts = [mm(x, joint).astype(BF16) for x, joint in zip(rounded, joints)]
        seconds = [mm(first, x) for first, x in zip(firsts, rounded)]
        inverses = [inverse - second for inverse, second in zip(inverses, seconds)]
    rests = [eye - inverse - mm3(lower, inverse) for lower, inverse in zip(lowers, inverses)]
    return [inverse + mm(inverse.astype(BF16), rest.astype(BF16)) for inverse, rest in zip(inverses, rests)]


def layer(
    devices,
    peers,
    repeat,
    tokens_ref,
    taps_query_key,
    taps_value,
    logd_ref,
    beta_ref,
    seg_ref,
    gain_ref,
    w_query_key_hbm,
    w_value_hbm,
    w_gate_hbm,
    w_output_hbm,
    out_ref,
    w_query_key,
    w_value,
    w_gate,
    w_output,
    gathered,
    tail_out,
    gate_ref,
    normed,
    ext,
    tail,
    level_ref,
    gam_ref,
    keys,
    decays,
    corrected,
    map_high,
    map_low,
    bmat,
    outgoing,
    incoming,
    entering,
    maps_out,
    maps_in,
    leads_out,
    leads_in,
    core_out,
    core_in,
    chip_out,
    chip_in,
    total,
    weight_sems,
    tail_sems,
    send_sems,
    recv_sems,
    far_send,
    maps_send,
    maps_recv,
    leads_send,
    leads_recv,
    gather_send,
    gather_recv,
    pass_send,
    pass_recv,
    core_send,
    core_recv,
    chip_send,
    chip_recv,
):
    me = lax.axis_index("ctx")
    slot = lax.axis_index("tp")
    core, chip, chips = slot % 2, slot // 2, peers // 2
    partner = chip * 2 + 1 - core
    not_first = me > 0
    not_last = me < devices - 1
    pair = me // 2
    odd = me % 2 == 1
    even = me % 2 == 0
    has_before = jnp.logical_and(odd, me > 2)
    opens = jnp.logical_and(odd, pair == 0)
    has_after = jnp.logical_and(odd, not_last)
    rows, depth = tokens_ref.shape
    count = rows * peers
    heads_v = logd_ref.shape[0]
    heads_k = heads_v // repeat
    width_qk = heads_k * DK
    width_v = heads_v * DV
    width = 2 * width_qk + width_v

    loads = [
        pltpu.make_async_copy(src, dst, weight_sems.at[n])
        for n, (src, dst) in enumerate(
            [
                (w_query_key_hbm, w_query_key),
                (w_value_hbm, w_value),
                (w_gate_hbm, w_gate),
                (w_output_hbm, w_output),
            ]
        )
    ]
    for load in loads:
        load.start()

    def chip_at(d):
        return lax.rem(chip + d, chips)

    def on_chip(d):
        return {"tp": chip_at(d) * 2 + core}

    barrier = pltpu.get_barrier_semaphore()

    @pl.when(not_first)
    def _():
        pl.semaphore_signal(barrier, inc=1, device_id={"ctx": me - 1}, device_id_type=MESH)

    @pl.when(not_last)
    def _():
        pl.semaphore_signal(barrier, inc=1, device_id={"ctx": me + 1}, device_id_type=MESH)

    @pl.when(has_before)
    def _():
        pl.semaphore_signal(barrier, inc=1, device_id={"ctx": me - 2}, device_id_type=MESH)

    @pl.when(has_after)
    def _():
        pl.semaphore_signal(barrier, inc=1, device_id={"ctx": me + 2}, device_id_type=MESH)

    pl.semaphore_signal(barrier, inc=1, device_id={"tp": partner}, device_id_type=MESH)
    for d in range(1, chips):
        pl.semaphore_signal(barrier, inc=1, device_id=on_chip(d), device_id_type=MESH)
    near = not_first.astype(jnp.int32) + not_last.astype(jnp.int32)
    far = has_before.astype(jnp.int32) + has_after.astype(jnp.int32)
    pl.semaphore_wait(barrier, near + far + chips)

    def remote(src, dst, send, recv, device):
        return pltpu.make_async_remote_copy(
            src_ref=src, dst_ref=dst, send_sem=send, recv_sem=recv, device_id=device, device_id_type=MESH
        )

    def block(index):
        return gathered.at[pl.ds(pl.multiple_of(index * rows, 16), rows)]

    across = [
        remote(tokens_ref, block(slot), gather_send.at[d], gather_recv.at[d], on_chip(d))
        for d in range(1, chips)
    ]
    for copy in across:
        copy.start()
    passes = [remote(tokens_ref, block(slot), pass_send.at[0], pass_recv.at[0], {"tp": partner})]
    passes[0].start()
    gathered[pl.ds(pl.multiple_of(slot * rows, 16), rows), :] = tokens_ref[...]

    level_ref[...] = level_of(HALF)
    upper = (iota((count, count), 0) <= iota((count, count), 1)).astype(F32)
    gam_ref[...] = lax.dot_general(
        logd_ref[...], upper, (((1,), (0,)), ((), ())), precision=lax.Precision.HIGHEST,
        preferred_element_type=F32,
    )

    for d in range(1, chips):
        across[d - 1].wait_recv()
        came = chip_at(chips - d) * 2 + core
        passes.append(remote(block(came), block(came), pass_send.at[d], pass_recv.at[d], {"tp": partner}))
        passes[d].start()
    for copy in passes:
        copy.wait_recv()

    def project_pre(weight, first, columns):
        def tile(t, carry):
            lanes = pl.ds(pl.multiple_of(t * TILE, TILE), TILE)
            to = pl.ds(pl.multiple_of(first + t * TILE, TILE), TILE)
            part = mm(gathered[...], weight[:, lanes]).astype(BF16)
            ext[TAIL:, to] = part.astype(F32)
            tail_out[:, to] = part[count - TAIL :]
            return carry

        lax.fori_loop(0, columns // TILE, tile, 0)

    loads[0].wait()
    project_pre(w_query_key.at[0], 0, width_qk)
    project_pre(w_query_key.at[1], width_qk, width_qk)
    loads[1].wait()
    project_pre(w_value, 2 * width_qk, width_v)

    tail_copy = remote(tail_out, tail, tail_sems.at[0], tail_sems.at[1], {"ctx": me + 1})

    @pl.when(not_last)
    def _():
        tail_copy.start()

    loads[2].wait()

    def project_gate(t, carry):
        lanes = pl.ds(pl.multiple_of(t * TILE, TILE), TILE)
        gate_ref[:, lanes] = mm(gathered[...], w_gate[:, lanes])
        return carry

    lax.fori_loop(0, width_v // TILE, project_gate, 0)

    @pl.when(jnp.logical_not(not_first))
    def _():
        ext[:TAIL, :] = jnp.zeros((TAIL, width), F32)

    @pl.when(not_first)
    def _():
        tail_copy.wait_recv()
        ext[:TAIL, :] = tail[...].astype(F32)

    offset = me * count
    seg_row = seg_ref[...].astype(F32)
    seg_col = column(seg_row)
    position = (offset + iota((count, 1), 0)).astype(F32)
    since = position - seg_col
    valids = [(since >= float(CONV - 1 - j)).astype(F32) for j in range(CONV)]
    enters = (seg_col < offset.astype(F32)).astype(F32)
    same_last = seg_col == jnp.max(seg_row, axis=1, keepdims=True)

    def conv(at, taps_ref, tap_at):
        lanes = pl.ds(pl.multiple_of(at, 128), 128)
        tap_lanes = pl.ds(pl.multiple_of(tap_at, 128), 128)
        total = None
        for j in range(CONV):
            term = ext[TAIL - (CONV - 1) + j : TAIL - (CONV - 1) + j + count, lanes] * (
                taps_ref[j : j + 1, tap_lanes] * valids[j]
            )
            total = term if total is None else total + term
        return silu(total)

    def unit(x):
        return x * lax.rsqrt(jnp.sum(x * x, axis=-1, keepdims=True) + 1e-06)

    def to_next(g):
        return remote(outgoing.at[g], incoming.at[g], send_sems.at[g], recv_sems.at[g], {"ctx": me + 1})

    def to_pair(g):
        return remote(outgoing.at[g], incoming.at[g], far_send.at[g], recv_sems.at[g], {"ctx": me + 2})

    def map_copies(g):
        to = {"ctx": me + 1}
        return (
            remote(maps_out.at[g], maps_in.at[g], maps_send.at[g], maps_recv.at[g], to),
            remote(leads_out.at[g], leads_in.at[g], leads_send.at[g], leads_recv.at[g], to),
        )

    def head_lanes(h):
        return pl.ds(pl.multiple_of(h * DV, 128), DV)

    span = DV + DK

    def join_maps(g):
        for copy in map_copies(g):
            copy.wait_recv()
        for sub in range(repeat):
            h = g * repeat + sub
            high, low = map_high[h], map_low[h]
            slab = maps_in[g, sub * span : (sub + 1) * span, :]
            product = mm(slab, high) + mm(slab, low)
            bmat[h] = bmat[h] + product[:DV]
            lead = leads_in[g, sub : sub + 1, :]
            map_high[h], map_low[h] = halves(lead * (high.astype(F32) + low.astype(F32)) - product[DV:])

    def pass_state(g):
        @pl.when(pair > 0)
        def _():
            to_pair(g).wait_recv()

        @pl.when(pair == 0)
        def _():
            incoming[g] = jnp.zeros((repeat * DV, DK), BF16)

        @pl.when(has_after)
        def _():
            for sub in range(repeat):
                h = g * repeat + sub
                part = slice(sub * DV, (sub + 1) * DV)
                state = incoming[g, part, :]
                outgoing[g, part, :] = (mm(state, map_high[h]) + mm(state, map_low[h]) + bmat[h]).astype(BF16)
            to_pair(g).start()
            to_next(g).start()

        @pl.when(odd)
        def _():
            for sub in range(repeat):
                part = slice(sub * DV, (sub + 1) * DV)
                state = incoming[g, part, :]
                b_slab = maps_in[g, sub * span : sub * span + DV, :]
                m_slab = maps_in[g, sub * span + DV : (sub + 1) * span, :]
                kept = leads_in[g, sub : sub + 1, :] * state.astype(F32)
                entering[g, part, :] = (kept - mm(state, m_slab) + b_slab.astype(F32)).astype(BF16)

        @pl.when(even)
        def _():
            entering[g] = incoming[g]

    ahead = jnp.minimum(jnp.where(odd, 1 + pair, heads_k), heads_k)
    eye = (iota((HALF, HALF), 0) == iota((HALF, HALF), 1)).astype(F32)
    parts = [slice(b * HALF, (b + 1) * HALF) for b in range(count // HALF)]

    def key_side(g, carry):
        key = unit(conv(width_qk + g * DK, taps_query_key.at[1], g * DK))
        key_b = key.astype(BF16)
        keys[:, head_lanes(g)] = key_b
        keys_dot = mm(key_b, key_b, ((1,), (1,)))
        rows_i, cols_i = iota((count, count), 0), iota((count, count), 1)
        within = jnp.logical_and(rows_i >= cols_i, seg_col == seg_row)
        strict = jnp.logical_and(rows_i > cols_i, within)
        level = level_ref[...]
        lowers, sides, lasts, leads = [], [], [], []
        for sub in range(repeat):
            h = g * repeat + sub
            value = conv(2 * width_qk + h * DV, taps_value, h * DV)
            gam_row = gam_ref[pl.ds(h, 1), :]
            gam_col = column(gam_row)
            beta_col = column(beta_ref[pl.ds(h, 1), :])
            decay = jnp.where(within, jnp.exp(jnp.where(within, gam_col - gam_row, 0.0)), 0.0)
            decays[h] = decay
            lead = jnp.exp(gam_col) * enters
            lowers.append(jnp.where(strict, beta_col * keys_dot * decay, 0.0))
            sides.append(jnp.concatenate([beta_col * value, (beta_col * lead) * key], axis=1))
            gam_last = gam_row[:, count - 1 :]
            lasts.append(jnp.where(same_last, jnp.exp(jnp.where(same_last, gam_last - gam_col, 0.0)), 0.0))
            leads.append(lead[count - 1 :, :])
        inverses = unit_lower_inverses([lower[r, r] for lower in lowers for r in parts], level, eye)
        solved = [[] for _ in range(repeat)]
        for b, r in enumerate(parts):
            for sub in range(repeat):
                part = sides[sub][r]
                if b:
                    part = part - mm3(lowers[sub][r, : b * HALF], jnp.concatenate(solved[sub], axis=0))
                solved[sub].append(mm3(inverses[sub * len(parts) + b], part))
        for sub in range(repeat):
            h = g * repeat + sub
            w_both = jnp.concatenate(solved[sub], axis=0)
            corrected[h] = w_both.astype(BF16)
            maps = mm((w_both * lasts[sub]).astype(BF16), key_b, ((0,), (0,)))
            bmat[h] = maps[:DV]
            map_high[h], map_low[h] = halves(leads[sub] * eye - maps[DV:])
            maps_out[g, sub * span : (sub + 1) * span, :] = maps.astype(BF16)
            leads_out[g, sub : sub + 1, :] = jnp.broadcast_to(leads[sub], (1, DK))

        @pl.when(even)
        def _():
            for copy in map_copies(g):
                copy.start()

        @pl.when(jnp.logical_and(odd, g >= 1))
        def _():
            join_maps(g - 1)

        @pl.when(g >= ahead)
        def _():
            pass_state(g - ahead)

        return carry

    lax.fori_loop(0, heads_k, key_side, 0)

    @pl.when(odd)
    def _():
        join_maps(heads_k - 1)

    @pl.when(opens)
    def _():
        pass_state(heads_k - 1)

    def query_side(g, carry):
        query = unit(conv(g * DK, taps_query_key.at[0], g * DK)) * DK ** (-0.5)
        query_dot = mm(query.astype(BF16), keys[:, head_lanes(g)], ((1,), (1,)))
        firsts, edges = [], []
        for sub in range(repeat):
            h = g * repeat + sub
            lead = jnp.exp(column(gam_ref[pl.ds(h, 1), :])) * enters
            both = mm((query_dot * decays[h]).astype(BF16), corrected[h])
            firsts.append(both[:, :DV])
            edges.append((lead * query - both[:, DV:]).astype(BF16))

        @pl.when(jnp.logical_and(g < ahead, jnp.logical_not(opens)))
        def _():
            pass_state(heads_k - ahead + g)

        for sub in range(repeat):
            lanes = head_lanes(g * repeat + sub)
            state = entering[g, sub * DV : (sub + 1) * DV, :]
            recur = firsts[sub] + mm(edges[sub], state, ((1,), (1,)))
            scale = lax.rsqrt(jnp.mean(recur * recur, axis=-1, keepdims=True) + 1e-06)
            normed[:, lanes] = (recur * scale * gain_ref[...] * silu(gate_ref[:, lanes])).astype(BF16)
        return carry

    lax.fori_loop(0, heads_k, query_side, 0)

    loads[3].wait()
    tiles = depth // OUT_TILE

    def rows_for(which):
        return jnp.concatenate(
            [
                normed[pl.ds(pl.multiple_of((chip_at(d) * 2 + which) * rows, 16), rows), :]
                for d in range(chips)
            ],
            axis=0,
        )

    def core_copy(t):
        return remote(core_out.at[t], core_in.at[t], core_send.at[t], core_recv.at[t], {"tp": partner})

    def chip_copy(t, d):
        return remote(
            chip_out.at[t, d - 1], chip_in.at[t, d - 1], chip_send.at[t, d - 1], chip_recv.at[t, d - 1], on_chip(d)
        )

    def for_partner(t, carry):
        lanes = pl.ds(pl.multiple_of(t * OUT_TILE, OUT_TILE), OUT_TILE)
        core_out[t] = mm(rows_for(1 - core), w_output[:, lanes]).astype(BF16)
        core_copy(t).start()
        return carry

    lax.fori_loop(0, tiles, for_partner, 0)

    def for_core(t, carry):
        lanes = pl.ds(pl.multiple_of(t * OUT_TILE, OUT_TILE), OUT_TILE)
        part = mm(rows_for(core), w_output[:, lanes])
        core_copy(t).wait_recv()
        part = part + core_in[t].astype(F32)
        for d in range(1, chips):
            chip_out[t, d - 1] = part[d * rows : (d + 1) * rows].astype(BF16)
            chip_copy(t, d).start()
        total[:, lanes] = part[:rows]
        return carry

    lax.fori_loop(0, tiles, for_core, 0)

    def finish(t, carry):
        lanes = pl.ds(pl.multiple_of(t * OUT_TILE, OUT_TILE), OUT_TILE)
        part = total[:, lanes]
        for d in range(1, chips):
            chip_copy(t, d).wait_recv()
            part = part + chip_in[t, d - 1].astype(F32)
        out_ref[:, lanes] = part.astype(BF16)
        return carry

    lax.fori_loop(0, tiles, finish, 0)

    for copy in across + passes:
        copy.wait_send()

    def drain_sums(t, carry):
        core_copy(t).wait_send()
        for d in range(1, chips):
            chip_copy(t, d).wait_send()
        return carry

    lax.fori_loop(0, tiles, drain_sums, 0)

    @pl.when(not_last)
    def _():
        tail_copy.wait_send()

    @pl.when(has_after)
    def _():
        def drain(g, carry):
            to_pair(g).wait_send()
            to_next(g).wait_send()
            return carry

        lax.fori_loop(0, heads_k, drain, 0)

    @pl.when(even)
    def _():
        def drain(g, carry):
            for copy in map_copies(g):
                copy.wait_send()
            return carry

        lax.fori_loop(0, heads_k, drain, 0)


def local(
    devices,
    peers,
    tokens,
    w_query_key,
    w_value,
    w_gate_out,
    conv_query_key,
    conv_value,
    log_decay,
    beta,
    seg_start,
    norm_gain,
    w_output,
):
    width_qk = w_query_key.shape[2]
    width_v = w_value.shape[1]
    heads_k = width_qk // DK
    heads_v = width_v // DV
    count = seg_start.shape[0]
    rows, depth = tokens.shape
    width = 2 * width_qk + width_v
    chips = peers // 2
    others = max(chips - 1, 1)
    tiles = depth // OUT_TILE
    vmem = pl.BlockSpec(memory_space=pltpu.VMEM)
    anywhere = pl.BlockSpec(memory_space=pl.ANY)
    dma = pltpu.SemaphoreType.DMA
    return pl.pallas_call(
        functools.partial(layer, devices, peers, heads_v // heads_k),
        out_shape=jax.ShapeDtypeStruct((rows, depth), BF16),
        in_specs=[vmem] * 7 + [anywhere] * 4,
        out_specs=vmem,
        scratch_shapes=[
            pltpu.VMEM(w_query_key.shape, BF16),
            pltpu.VMEM(w_value.shape, BF16),
            pltpu.VMEM(w_gate_out.shape, BF16),
            pltpu.VMEM(w_output.shape, BF16),
            pltpu.VMEM((count, depth), BF16),
            pltpu.VMEM((TAIL, width), BF16),
            pltpu.VMEM((count, width_v), F32),
            pltpu.VMEM((count, width_v), BF16),
            pltpu.VMEM((TAIL + count, width), F32),
            pltpu.VMEM((TAIL, width), BF16),
            pltpu.VMEM((HALF, HALF), jnp.int32),
            pltpu.VMEM((heads_v, count), F32),
            pltpu.VMEM((count, width_qk), BF16),
            pltpu.VMEM((heads_v, count, count), F32),
            pltpu.VMEM((heads_v, count, DV + DK), BF16),
            pltpu.VMEM((heads_v, DK, DK), BF16),
            pltpu.VMEM((heads_v, DK, DK), BF16),
            pltpu.VMEM((heads_v, DV, DK), F32),
            pltpu.VMEM((heads_k, heads_v // heads_k * DV, DK), BF16),
            pltpu.VMEM((heads_k, heads_v // heads_k * DV, DK), BF16),
            pltpu.VMEM((heads_k, heads_v // heads_k * DV, DK), BF16),
            pltpu.VMEM((heads_k, heads_v // heads_k * (DV + DK), DK), BF16),
            pltpu.VMEM((heads_k, heads_v // heads_k * (DV + DK), DK), BF16),
            pltpu.VMEM((heads_k, 8, DK), F32),
            pltpu.VMEM((heads_k, 8, DK), F32),
            pltpu.VMEM((tiles, chips * rows, OUT_TILE), BF16),
            pltpu.VMEM((tiles, chips * rows, OUT_TILE), BF16),
            pltpu.VMEM((tiles, others, rows, OUT_TILE), BF16),
            pltpu.VMEM((tiles, others, rows, OUT_TILE), BF16),
            pltpu.VMEM((rows, depth), F32),
            dma((4,)),
            dma((2,)),
            dma((heads_k,)),
            dma((heads_k,)),
            dma((heads_k,)),
            dma((heads_k,)),
            dma((heads_k,)),
            dma((heads_k,)),
            dma((heads_k,)),
            dma((chips,)),
            dma((chips,)),
            dma((chips,)),
            dma((chips,)),
            dma((tiles,)),
            dma((tiles,)),
            dma((tiles, others)),
            dma((tiles, others)),
        ],
        compiler_params=pltpu.CompilerParams(
            collective_id=0, has_side_effects=True, vmem_limit_bytes=56 << 20
        ),
    )(
        tokens,
        conv_query_key,
        conv_value,
        log_decay,
        beta,
        seg_start.reshape(1, count),
        norm_gain.reshape(1, DV),
        w_query_key,
        w_value,
        w_gate_out,
        w_output,
    )


def solution(mesh):
    return jax.shard_map(
        functools.partial(local, mesh.shape["ctx"], mesh.shape["tp"]),
        mesh=mesh,
        in_specs=(
            P(("ctx", "tp"), None),
            P(None, None, "tp"),
            P(None, "tp"),
            P(None, "tp"),
            P(None, None, "tp"),
            P(None, "tp"),
            P("tp", "ctx"),
            P("tp", "ctx"),
            P("ctx"),
            P(),
            P("tp", None),
        ),
        out_specs=P(("ctx", "tp"), None),
        check_vma=False,
    )
```
